32 devices in a mesh: group: 4 (over y, x), det: 4 (over z), tm: 2 (over core).
Axes of the slice: x: 2, y: 2, z: 4, core: 2. Of those that a mesh axis runs over, the one named last changes fastest.
Arguments:
- map_solution: float32 [3, 4, 64, 128], P(None, 'det', ('group', 'tm')), may hold values from -6 to 6
- map_residual: float32 [3, 4, 64, 128], P(None, 'det', ('group', 'tm')), may hold values from -6 to 6
- map_direction: float32 [3, 4, 64, 128], P(None, 'det', ('group', 'tm')), may hold values from -6 to 6
- hits: int32 [256, 256], P(('group', 'det'), 'tm'), may hold values from 0 to 192, as said below
- stokes_int: int32 [2, 256, 32768], P(None, ('group', 'det'), 'tm'), may hold values from -2047 to 2047
- inv_noise: float32 [256, 512], P(('group', 'det')), may hold values from 0.2 to 2
Outputs:
- new_solution: float32 [3, 4, 64, 128], P(None, 'det', ('group', 'tm'))
- new_residual: float32 [3, 4, 64, 128], P(None, 'det', ('group', 'tm'))
- new_direction: float32 [3, 4, 64, 128], P(None, 'det', ('group', 'tm'))
The draws below stay inside these ranges and needn't reach their ends.
Inputs may be any that keep to these rules, and one draw needn't show every extreme that they name: `hits`: A value below 192 names a pixel block in the sky tile of the detector's det index or in one of its two neighbours along det, as the steps say; the value 192 marks a flagged block.
All inputs are finite; a program needn't handle non-finite values.
Results may differ from the reference program's by a relative error of at most 0.0003.
Values sent between devices are 32-bit elements; how exact they have to be, the bound alone decides.
No kernel may reach another device: no remote copies, remote signals or barrier semaphores. Data moves between devices by JAX's collectives and lax.ppermute only.
A program may use at most 64 MiB of HBM per device.

```python
import math
import jax
import jax.numpy as jnp
from jax import lax

DET_DEV = 16
WIN = 1024
FREQS = 512
DETS = 256
SAMPLES = 32768
BLOCKS = 256
TILES = 4
TILE_PB = 64
LOCAL = 192


def draw_hits(key, part):
    first_key, second_key = jax.random.split(jax.random.fold_in(key, 11))
    blocks = jax.random.randint(first_key, (DETS, BLOCKS), 0, LOCAL)
    flagged = jax.random.randint(second_key, (DETS, BLOCKS), 0, 8) == 0
    result = jnp.where(flagged, LOCAL, blocks)
    result = result.at[0, 0].set(LOCAL).at[0, 1].set(0)
    return result.astype(jnp.int32)


def set_ends(array, own_key, smallest, top_value):
    place = [jax.random.randint(jax.random.fold_in(own_key, axis), (), 0, length) for axis, length in enumerate(array.shape)]
    widest = array.shape.index(max(array.shape))
    next_to = place[:widest] + [(place[widest] + 1) % array.shape[widest]] + place[widest + 1:]
    return array.at[tuple(place)].set(smallest).at[tuple(next_to)].set(top_value)


def level_of(key, extent, shards, low, top_value):
    factor_of, own = 1.0, jax.random.fold_in(key, 6)
    for axis_at, parts in shards:
        draws = jnp.exp(jax.random.uniform(jax.random.fold_in(own, axis_at), (parts,), jnp.float32, low / len(shards), top_value / len(shards)))
        factor_of = factor_of * jnp.repeat(draws, extent[axis_at] // parts).reshape([-1 if axis == axis_at else 1 for axis in range(len(extent))])
    return factor_of


def scatter_about(stream_key, dims, width, reach, cuts=(), held_as=jnp.bfloat16):
    values = jax.random.normal(stream_key, dims, jnp.float32) * width
    if len(cuts) > 0:
        values = level_of(stream_key, dims, cuts, -0.22, 0.18) * values
    return jnp.clip(values, min=-reach, max=reach).astype(held_as)


def setup_inputs(seed: int = 0) -> dict:
    seeds = jax.random.split(jax.random.key(seed), 7)
    return {
        "map_solution": scatter_about(seeds[0], (3, TILES, TILE_PB, 128), 1.0, 6.0, ((1, 4), (2, 8)), jnp.float32),
        "map_residual": scatter_about(seeds[1], (3, TILES, TILE_PB, 128), 1.0, 6.0, ((1, 4), (2, 8)), jnp.float32),
        "map_direction": scatter_about(seeds[2], (3, TILES, TILE_PB, 128), 1.0, 6.0, ((1, 4), (2, 8)), jnp.float32),
        "hits": draw_hits(jax.random.fold_in(seeds[6], 71), 0),
        "stokes_int": set_ends(jax.random.randint(seeds[4], (2, DETS, SAMPLES), -2047, 2048), jax.random.fold_in(seeds[4], 1), -2047, 2047).astype(jnp.int32),
        "inv_noise": jnp.clip(jnp.exp(math.log(2.0) - 2.3025851 * jax.random.uniform(seeds[5], (DETS, FREQS), jnp.float32) ** level_of(seeds[5], (DETS, FREQS), ((0, 16),), -0.2, 0.2)), 0.2, 2.0),
    }


def basis_rows(length):
    row_ids = jnp.arange(length, dtype=jnp.int32)[:, None]
    sample_ids = jnp.arange(length, dtype=jnp.int32)[None, :]
    middle = length // 2
    frequency = jnp.where(row_ids <= middle, row_ids, row_ids - middle)
    phases = frequency * sample_ids % length
    angles = phases.astype(jnp.float32) * (2.0 * math.pi / length)
    values = jnp.where(row_ids > middle, jnp.sin(angles), jnp.cos(angles))
    scales = jnp.where((row_ids == 0) | (row_ids == middle), math.sqrt(1.0 / length), math.sqrt(2.0 / length))
    return values * scales

def noise_filter(extended, spectrum, basis_table):
    row_count = extended.shape[0]
    length = basis_table.shape[0]
    segment = length // 2
    pieces = extended.reshape(row_count, -1, segment)
    windows = jnp.concatenate([pieces[:, :-1], pieces[:, 1:]], axis=2)
    windows_count = windows.shape[1]
    weights = jnp.concatenate([spectrum, spectrum[:, -1:], spectrum[:, 1:]], axis=1)
    coeffs = jnp.dot(windows.reshape(-1, length), basis_table.T, precision=lax.Precision.HIGHEST)
    coeffs = coeffs.reshape(row_count, windows_count, length) * weights[:, None, :]
    restored = jnp.dot(coeffs.reshape(-1, length), basis_table, precision=lax.Precision.HIGHEST)
    restored = restored.reshape(row_count, windows_count, length)
    return (restored[:, :-1, segment:] + restored[:, 1:, :segment]).reshape(row_count, -1)

def reference(map_solution, map_residual, map_direction, hits, stokes_int, inv_noise):
    basis_table = basis_rows(WIN)
    segment = WIN // 2
    pixels = TILES * TILE_PB
    flat_direction = jnp.concatenate([map_direction.reshape(3, pixels, 128), jnp.zeros((3, 1, 128), jnp.float32)], axis=1)

    def one_block(binned, block_index):
        row_start = (block_index * DET_DEV).astype(jnp.int32)
        block_hits = lax.dynamic_slice_in_dim(hits, row_start, DET_DEV, 0)
        sky_tile = block_index % TILES
        tile_ids = (sky_tile + block_hits // TILE_PB - 1) % TILES
        indices = jnp.where(block_hits == LOCAL, pixels, tile_ids * TILE_PB + block_hits % TILE_PB).reshape(-1).astype(jnp.int32)
        weights_int = lax.dynamic_slice_in_dim(stokes_int, row_start, DET_DEV, 1)
        q_weight = (weights_int[0].astype(jnp.float32) / 2048.0).reshape(-1, 128)
        u_weight = (weights_int[1].astype(jnp.float32) / 2048.0).reshape(-1, 128)
        picked = jnp.take(flat_direction, indices, axis=1)
        scanned = (picked[0] + q_weight * picked[1] + u_weight * picked[2]).reshape(DET_DEV, SAMPLES)
        extended = jnp.pad(scanned, ((0, 0), (segment, segment)))
        spectrum = lax.dynamic_slice_in_dim(inv_noise, row_start, DET_DEV, 0)
        filtered = noise_filter(extended, spectrum, basis_table).reshape(-1, 128)
        block_terms = jnp.stack([jax.ops.segment_sum(values, indices, num_segments=pixels + 1) for values in (filtered, q_weight * filtered, u_weight * filtered)])
        return (binned + block_terms, None)
    binned, ignored = lax.scan(one_block, jnp.zeros((3, pixels + 1, 128), jnp.float32), jnp.arange(DETS // DET_DEV, dtype=jnp.int32))
    map_image = binned[:, :pixels].reshape(3, TILES, TILE_PB, 128)
    old_norm = jnp.sum(map_residual * map_residual)
    curvature = jnp.sum(map_direction * map_image)
    step_size = old_norm / curvature
    new_solution = map_solution + step_size * map_direction
    new_residual = map_residual - step_size * map_image
    new_norm = jnp.sum(new_residual * new_residual)
    new_direction = new_residual + new_norm / old_norm * map_direction
    return (new_solution, new_residual, new_direction)
```

```python
import functools
import math

import jax
import jax.numpy as jnp
import numpy as np
from jax import lax
from jax.experimental import pallas as pl
from jax.experimental.pallas import tpu as pltpu
from jax.sharding import PartitionSpec as P

WIN = 1024
LANES = 128
SEG = WIN // 2
HALF = SEG // 2
PER_SEG = SEG // LANES
BF = jnp.bfloat16
F32 = jnp.float32


def split(value):
    high = value.astype(BF)
    return high, (value - high.astype(F32)).astype(BF)


def np_split(value):
    value = np.asarray(value, np.float32)
    high = value.astype(jnp.bfloat16)
    return high, (value - high.astype(np.float32)).astype(jnp.bfloat16)


def trig_table(samples, frequencies, length, with_ends):
    n = np.arange(samples)[:, None]
    cos_f = np.asarray(frequencies)
    sin_f = np.asarray([f for f in frequencies if not (with_ends and f in (0, length // 2))])
    angle = 2.0 * math.pi / length
    cos_t = np.cos(angle * ((n * cos_f[None, :]) % length))
    sin_t = np.sin(angle * ((n * sin_f[None, :]) % length))
    scale = np.full(len(cos_f), math.sqrt(2.0 / samples))
    if with_ends:
        scale[(cos_f == 0) | (cos_f == length // 2)] = math.sqrt(1.0 / samples)
    return np.concatenate([cos_t * scale, sin_t * math.sqrt(2.0 / samples)], axis=1), np.concatenate([cos_f, sin_f])


def tables():
    ee, ee_f = trig_table(HALF, np.arange(0, SEG + 1, 4), WIN, True)
    eo, eo_f = trig_table(HALF, np.arange(2, SEG, 4), WIN, False)
    od, od_f = trig_table(SEG, np.arange(1, SEG, 2), WIN, False)
    return (ee, ee_f), (eo, eo_f), (od, od_f)


def dot(a, b):
    return lax.dot_general(a, b, (((1,), (0,)), ((), ())), preferred_element_type=F32)


def dot_t(a, b):
    return lax.dot_general(a, b, (((1,), (1,)), ((), ())), preferred_element_type=F32)


def dot3(op, value, high, low):
    vh, vl = split(value)
    return op(vh, high) + (op(vl, high) + op(vh, low))


def main_kernel(
    groups, times, low, own, high, hits, stokes, left, right, wee, weo, wod,
    g1h, g1l, g2h, g2l, sh, sl, out, mh, ml, onehot, x, f,
):
    rows, blocks = hits.shape
    tile_blocks = own.shape[1]
    local = 3 * tile_blocks
    depth = mh.shape[0]
    segs = blocks // PER_SEG
    chunk_segs = 4
    chunk_blocks = chunk_segs * PER_SEG
    chunk = chunk_blocks * rows
    scale = 1.0 / 2048.0

    if depth > local:
        mh[pl.ds(local, depth - local), :] = jnp.zeros((depth - local, 3 * LANES), BF)
        ml[pl.ds(local, depth - local), :] = jnp.zeros((depth - local, 3 * LANES), BF)
    for t, ref in enumerate((low, own, high)):
        for c in range(3):
            part_h, part_l = split(ref[c])
            mh[pl.ds(t * tile_blocks, tile_blocks), pl.ds(c * LANES, LANES)] = part_h
            ml[pl.ds(t * tile_blocks, tile_blocks), pl.ds(c * LANES, LANES)] = part_l

    ids = lax.broadcasted_iota(jnp.int32, (rows, depth), 1)

    def rows_of(column):
        return jnp.where(jnp.broadcast_to(column, (rows, depth)) == ids, 1.0, 0.0).astype(BF)

    def scan(picked, j, q_int, u_int):
        part = picked[j * rows:(j + 1) * rows]
        q = q_int.astype(F32) * scale
        u = u_int.astype(F32) * scale
        return part[:, :LANES] + q * part[:, LANES:2 * LANES] + u * part[:, 2 * LANES:]

    for side, at in ((left, 0), (right, (segs + 1) * rows)):
        flags = side[:, 2 * SEG:] - 1
        ones = jnp.concatenate([rows_of(flags[:, j:j + 1]) for j in range(PER_SEG)], axis=0)
        picked = dot(ones, mh[...]) + dot(ones, ml[...])
        for j in range(PER_SEG):
            x[pl.ds(at, rows), pl.ds(j * LANES, LANES)] = scan(
                picked, j, side[:, j * LANES:(j + 1) * LANES],
                side[:, SEG + j * LANES:SEG + (j + 1) * LANES],
            )

    def scan_chunk(i, carry):
        turned = pltpu.roll(hits[...], blocks - i * chunk_blocks, 1)
        ones = jnp.concatenate([rows_of(turned[:, j:j + 1]) for j in range(chunk_blocks)], axis=0)
        onehot[pl.ds(pl.multiple_of(i * chunk, chunk), chunk), :] = ones
        picked = dot(ones, mh[...]) + dot(ones, ml[...])
        for j in range(chunk_blocks):
            lanes = pl.ds(pl.multiple_of(i * chunk_blocks * LANES, LANES) + j * LANES, LANES)
            at = pl.multiple_of((i * chunk_segs + 1 + j // PER_SEG) * rows, rows)
            x[pl.ds(at, rows), pl.ds((j % PER_SEG) * LANES, LANES)] = scan(
                picked, j, stokes[0, :, lanes], stokes[1, :, lanes]
            )
        return carry

    lax.fori_loop(0, segs // chunk_segs, scan_chunk, 0)

    part_segs = 16
    part = part_segs * rows

    def weighted(coeffs, weights):
        return (coeffs.reshape(part_segs, rows, -1) * weights[...][None]).reshape(part, -1)

    def filter_part(i, carry):
        at = pl.multiple_of(i * part, part)
        middle = x[pl.ds(at + rows, part), :]
        around = 0.5 * (x[pl.ds(at, part), :] + x[pl.ds(at + 2 * rows, part), :])
        even = middle + around
        odd = middle - around
        coeffs = weighted(dot3(dot, even[:, :HALF] + even[:, HALF:], g1h[...], g1l[...]), wee)
        first = dot3(dot_t, coeffs, g1h[...], g1l[...])
        coeffs = weighted(dot3(dot, even[:, :HALF] - even[:, HALF:], g2h[...], g2l[...]), weo)
        second = dot3(dot_t, coeffs, g2h[...], g2l[...])
        coeffs = weighted(dot3(dot, odd, sh[...], sl[...]), wod)
        third = dot3(dot_t, coeffs, sh[...], sl[...])
        f[pl.ds(at, part), :HALF] = first + second + third[:, :HALF]
        f[pl.ds(at, part), HALF:] = first - second + third[:, HALF:]
        return carry

    lax.fori_loop(0, segs // part_segs, filter_part, 0)

    def bin_chunk(i, total):
        values = []
        for j in range(chunk_blocks):
            lanes = pl.ds(pl.multiple_of(i * chunk_blocks * LANES, LANES) + j * LANES, LANES)
            at = pl.multiple_of((i * chunk_segs + j // PER_SEG) * rows, rows)
            value = f[pl.ds(at, rows), pl.ds((j % PER_SEG) * LANES, LANES)]
            q = stokes[0, :, lanes].astype(F32) * scale
            u = stokes[1, :, lanes].astype(F32) * scale
            values.append(jnp.concatenate([value, q * value, u * value], axis=1))
        vh, vl = split(jnp.concatenate(values, axis=0))
        ones = onehot[pl.ds(pl.multiple_of(i * chunk, chunk), chunk), :]
        over = (((0,), (0,)), ((), ()))
        return total + (
            lax.dot_general(ones, vh, over, preferred_element_type=F32)
            + lax.dot_general(ones, vl, over, preferred_element_type=F32)
        )

    total = lax.fori_loop(0, segs // chunk_segs, bin_chunk, jnp.zeros((depth, 3 * LANES), F32))
    width = tile_blocks // (groups * times)
    for t in range(3):
        for g in range(groups):
            for k in range(times):
                start = t * tile_blocks + (g * times + k) * width
                out[k, t, g] = total[start:start + width]


def scan_filter_bin(low, own, high, hits, stokes, left, right, inv_noise, groups, times):
    rows, samples = stokes.shape[1:]
    blocks = samples // LANES
    tile_blocks = own.shape[1]
    depth = -(-3 * tile_blocks // 256) * 256
    (ee, ee_f), (eo, eo_f), (od, od_f) = tables()
    g1h, g1l = np_split(ee)
    g2h, g2l = np_split(eo)
    sh, sl = np_split(od)
    last = inv_noise.shape[1] - 1
    wee = 0.5 * jnp.concatenate([inv_noise[:, 0::4], inv_noise[:, last:], inv_noise[:, 4::4]], axis=1)
    weo = 0.5 * jnp.concatenate([inv_noise[:, 2::4], inv_noise[:, 2::4]], axis=1)
    wod = jnp.concatenate([inv_noise[:, 1::2], inv_noise[:, 1::2]], axis=1)
    width = tile_blocks // (groups * times)
    vmem = pl.BlockSpec(memory_space=pltpu.VMEM)
    return pl.pallas_call(
        functools.partial(main_kernel, groups, times),
        out_shape=jax.ShapeDtypeStruct((times, 3, groups, width, 3 * LANES), F32),
        in_specs=[vmem] * 16,
        out_specs=vmem,
        scratch_shapes=[
            pltpu.VMEM((depth, 3 * LANES), BF),
            pltpu.VMEM((depth, 3 * LANES), BF),
            pltpu.VMEM((rows * blocks, depth), BF),
            pltpu.VMEM(((blocks // PER_SEG + 2) * rows, SEG), F32),
            pltpu.VMEM((blocks // PER_SEG * rows, SEG), F32),
        ],
        compiler_params=pltpu.CompilerParams(vmem_limit_bytes=48 * 2**20),
    )(low, own, high, hits, stokes, left, right, wee, weo, wod, g1h, g1l, g2h, g2l, sh, sl)


def turned(axis, by):
    count = lax.axis_size(axis)
    return [(i, (i + by) % count) for i in range(count)]


def scatter_sum(parts, axis):
    count = lax.axis_size(axis)
    me = lax.axis_index(axis)
    total = lax.dynamic_index_in_dim(parts, me, 0, keepdims=False)
    for by in range(1, count):
        sent = lax.dynamic_index_in_dim(parts, (me + by) % count, 0, keepdims=False)
        total = total + lax.ppermute(sent, axis, turned(axis, by))
    return total


def direct_sum(value, axis):
    total = value
    for by in range(1, lax.axis_size(axis)):
        total = total + lax.ppermute(value, axis, turned(axis, by))
    return total


def edge(stokes_int, hits, end):
    if end:
        stokes, flags = stokes_int[:, :, -SEG:], hits[:, -PER_SEG:]
    else:
        stokes, flags = stokes_int[:, :, :SEG], hits[:, :PER_SEG]
    flags = jnp.pad(flags + 1, ((0, 0), (0, LANES - PER_SEG)))
    return jnp.concatenate([stokes[0], stokes[1], flags], axis=1)


def shards(map_solution, map_residual, map_direction, hits, stokes_int, inv_noise):
    times = lax.axis_size("tm")
    groups = lax.axis_size("group")
    forward = [(i, i + 1) for i in range(times - 1)]
    left = lax.ppermute(edge(stokes_int, hits, True), "tm", forward)
    right = lax.ppermute(edge(stokes_int, hits, False), "tm", [(b, a) for a, b in forward])
    tile = lax.all_gather(map_direction, ("group", "tm"), axis=2, tiled=True)[:, 0]
    low = lax.ppermute(tile, "det", turned("det", 1))
    high = lax.ppermute(tile, "det", turned("det", -1))
    binned = scan_filter_bin(low, tile, high, hits, stokes_int, left, right, inv_noise, groups, times)
    half = scatter_sum(binned, "tm")
    image = (
        half[1]
        + lax.ppermute(half[2], "det", turned("det", 1))
        + lax.ppermute(half[0], "det", turned("det", -1))
    )
    image = scatter_sum(image, "group")
    map_image = jnp.stack([image[:, c * LANES:(c + 1) * LANES] for c in range(3)])[:, None]
    sums = jnp.stack([
        jnp.sum(map_residual * map_residual),
        jnp.sum(map_direction * map_image),
        jnp.sum(map_residual * map_image),
        jnp.sum(map_image * map_image),
    ])
    for axis in ("tm", "group", "det"):
        sums = direct_sum(sums, axis)
    old_norm, curvature, cross_term, image_norm = sums
    step_size = old_norm / curvature
    new_residual = map_residual - step_size * map_image
    new_norm = old_norm - 2.0 * step_size * cross_term + step_size * step_size * image_norm
    new_solution = map_solution + step_size * map_direction
    new_direction = new_residual + new_norm / old_norm * map_direction
    return (new_solution, new_residual, new_direction)


def solution(mesh):
    map_placed = P(None, "det", ("group", "tm"), None)
    placed = (
        map_placed,
        map_placed,
        map_placed,
        P(("group", "det"), "tm"),
        P(None, ("group", "det"), "tm"),
        P(("group", "det"), None),
    )
    return jax.shard_map(
        shards,
        mesh=mesh,
        in_specs=placed,
        out_specs=(map_placed, map_placed, map_placed),
        check_vma=False,
    )
```

```python
import functools
import math

import jax
import jax.numpy as jnp
import numpy as np
from jax import lax
from jax.experimental import pallas as pl
from jax.experimental.pallas import tpu as pltpu
from jax.sharding import PartitionSpec as P

WIN = 1024
LANES = 128
SEG = WIN // 2
HALF = SEG // 2
PER_SEG = SEG // LANES
BF = jnp.bfloat16
F32 = jnp.float32


def split(value):
    high = value.astype(BF)
    return high, (value - high.astype(F32)).astype(BF)


def np_split(value):
    value = np.asarray(value, np.float32)
    high = value.astype(jnp.bfloat16)
    return high, (value - high.astype(np.float32)).astype(jnp.bfloat16)


def trig_table(samples, frequencies, length, with_ends):
    n = np.arange(samples)[:, None]
    cos_f = np.asarray(frequencies)
    sin_f = np.asarray([f for f in frequencies if not (with_ends and f in (0, length // 2))])
    angle = 2.0 * math.pi / length
    cos_t = np.cos(angle * ((n * cos_f[None, :]) % length))
    sin_t = np.sin(angle * ((n * sin_f[None, :]) % length))
    scale = np.full(len(cos_f), math.sqrt(2.0 / samples))
    if with_ends:
        scale[(cos_f == 0) | (cos_f == length // 2)] = math.sqrt(1.0 / samples)
    return np.concatenate([cos_t * scale, sin_t * math.sqrt(2.0 / samples)], axis=1)


def tables():
    ee = trig_table(HALF, np.arange(0, SEG + 1, 4), WIN, True)
    eo = trig_table(HALF, np.arange(2, SEG, 4), WIN, False)
    odd = trig_table(SEG, np.arange(1, SEG, 2), WIN, False)
    return ee, eo, odd


def dot(a, b):
    return lax.dot_general(a, b, (((1,), (0,)), ((), ())), preferred_element_type=F32)


def dot_t(a, b):
    return lax.dot_general(a, b, (((1,), (1,)), ((), ())), preferred_element_type=F32)


def partner_perm(axis, by):
    count = lax.axis_size(axis)
    if count & (count - 1) == 0:
        return [(i, i ^ by) for i in range(count)]
    return [(i, (i + by) % count) for i in range(count)]


def source_of(axis, by):
    count = lax.axis_size(axis)
    me = lax.axis_index(axis)
    if count & (count - 1) == 0:
        return me ^ by
    return lax.rem(me + count - by, count)


def target_of(axis, by):
    count = lax.axis_size(axis)
    me = lax.axis_index(axis)
    if count & (count - 1) == 0:
        return me ^ by
    return lax.rem(me + by, count)


def tile_perm(exchange):
    count = lax.axis_size("det")
    if count % 2:
        return [(i, (i + 1 - 2 * exchange) % count) for i in range(count)]
    pairs = [(i, (i + 1) % count) for i in range(1 - exchange, count, 2)]
    return sorted(pairs + [(b, a) for a, b in pairs])


def tile_sides(exchange):
    if lax.axis_size("det") % 2:
        return 2 * exchange, 2 - 2 * exchange
    odd = lax.rem(lax.axis_index("det"), 2)
    side = 2 * odd if exchange == 0 else 2 - 2 * odd
    return side, side


def dot3(op, value, high, low):
    vh, vl = split(value)
    return op(vh, high) + (op(vl, high) + op(vh, low))


def edge_kernel(count, hits, stokes, residual, *refs):
    edges_out, residual_out, raw, sems = refs[:count], refs[count], refs[count + 1], refs[count + 2]
    rows, blocks = hits.shape
    samples = stokes.shape[2]
    first = [lax.axis_index("tm") == 1] if count == 1 else [True, False]
    copies = []
    for i in range(count):
        at = jnp.where(first[i], 0, samples - SEG)
        lanes = pl.ds(pl.multiple_of(at, SEG), SEG)
        copies.append(pltpu.make_async_copy(stokes.at[:, :, lanes], raw.at[i], sems.at[i]))
        copies[i].start()
    residual_out[...] = residual[:, 0]
    flags = hits[...].astype(F32) + 1.0
    last_flags = pltpu.roll(flags, PER_SEG, 1)
    for i in range(count):
        edges_out[i][2 * PER_SEG] = jnp.where(first[i], flags, last_flags)
    for i in range(count):
        copies[i].wait()
        for k in range(2):
            for j in range(PER_SEG):
                part = raw[i, k, :, j * LANES:(j + 1) * LANES]
                edges_out[i][k * PER_SEG + j] = part.astype(F32) * (1.0 / 2048.0)


def prep_kernel(
    payload, hits, inv_noise, stokes, tables_in,
    payload_out, weights, onehot, scales, tables_out, raw, sems,
):
    rows, blocks = hits.shape
    depth = onehot.shape[1]
    parts = raw.shape[0]
    width = stokes.shape[2] // parts
    copies = [
        pltpu.make_async_copy(stokes.at[:, :, pl.ds(i * width, width)], raw.at[i], sems.at[i])
        for i in range(parts)
    ]
    copies.append(pltpu.make_async_copy(tables_in, tables_out, sems.at[parts]))
    for copy in copies:
        copy.start()
    payload_out[...] = payload[...]
    ids = lax.broadcasted_iota(jnp.int32, (rows, depth), 1)
    step = 16

    def ones_of(i, carry):
        part = pltpu.roll(hits[...], blocks - i * step, 1)
        for j in range(step):
            column = jnp.broadcast_to(part[:, j:j + 1], (rows, depth))
            at = pl.multiple_of((i * step + j) * rows, rows)
            onehot[pl.ds(at, rows), :] = jnp.where(column == ids, 1.0, 0.0).astype(BF)
        return carry

    lax.fori_loop(0, blocks // step, ones_of, 0)

    freqs = inv_noise.shape[1]
    column = lax.broadcasted_iota(jnp.int32, (1, WIN), 1)
    quarter = HALF // 2
    wanted = jnp.where(
        column < HALF,
        jnp.where(column <= quarter, 4 * column, 4 * (column - quarter)),
        jnp.where(
            column < SEG,
            4 * lax.rem(column, quarter) + 2,
            2 * lax.rem(column, HALF) + 1,
        ),
    )
    wanted = jnp.broadcast_to(jnp.minimum(wanted, freqs - 1), (freqs, WIN))
    held = lax.broadcasted_iota(jnp.int32, (freqs, WIN), 0)
    chosen = jnp.where(wanted == held, 1.0, 0.0).astype(BF)
    both = dot(jnp.concatenate(split(inv_noise[...]), axis=0), chosen)
    scales[...] = both[:rows] + both[rows:]

    for i in range(parts):
        copies[i].wait()
        for k in range(2):
            weights[k, :, pl.ds(i * width, width)] = raw[i, k].astype(F32) * (1.0 / 2048.0)
    copies[parts].wait()


def main_kernel(
    arrived, others, weights, onehot, scales, tables_in, *refs,
):
    sides, (out, window, mh, ml, x, f, total) = refs[:-7], refs[-7:]
    groups = lax.axis_size("group")
    times = lax.axis_size("tm")
    width = arrived.shape[3]
    rows = weights.shape[1]
    blocks = weights.shape[2] // LANES
    tile_blocks = groups * times * width
    depth = mh.shape[0]
    segs = blocks // PER_SEG
    chunk_segs = 4
    chunk_blocks = chunk_segs * PER_SEG
    chunk = chunk_blocks * rows
    tiles = (1, tile_sides(0)[0], tile_sides(1)[0])

    window[...] = jnp.zeros(window.shape, F32)
    for k in range(times):
        for j in range(groups):
            at = (source_of("group", j) * times + source_of("tm", k)) * width
            for s in range(3):
                place = pl.ds(pl.multiple_of(tiles[s] * tile_blocks + at, 8), width)
                for c in range(3):
                    piece = arrived[j, s, c] if k == 0 else others[k - 1, j, s, c]
                    window[place, pl.ds(c * LANES, LANES)] = piece
    mh[...], ml[...] = split(window[...])

    ids = lax.broadcasted_iota(jnp.int32, (rows, depth), 1).astype(F32)

    def scan(picked, j, q, u):
        part = picked[j * rows:(j + 1) * rows]
        return part[:, :LANES] + q * part[:, LANES:2 * LANES] + u * part[:, 2 * LANES:]

    upper_at = (segs + 1) * rows
    for at in (0, upper_at):
        x[pl.ds(at, rows), :] = jnp.zeros((rows, SEG), F32)
    if len(sides) == 1:
        places = (jnp.where(lax.axis_index("tm") == 0, upper_at, 0),)
    else:
        places = (0, upper_at)
    for side, at in zip(sides, places):
        flags = side[2 * PER_SEG] - 1.0
        ones = jnp.concatenate(
            [
                jnp.where(jnp.broadcast_to(flags[:, j:j + 1], (rows, depth)) == ids, 1.0, 0.0)
                for j in range(PER_SEG)
            ],
            axis=0,
        ).astype(BF)
        picked = dot(ones, mh[...]) + dot(ones, ml[...])
        place = pl.ds(at if isinstance(at, int) else pl.multiple_of(at, rows), rows)
        for j in range(PER_SEG):
            x[place, pl.ds(j * LANES, LANES)] = scan(picked, j, side[j], side[PER_SEG + j])

    def scan_chunk(i, carry):
        ones = onehot[pl.ds(pl.multiple_of(i * chunk, chunk), chunk), :]
        picked = dot(ones, mh[...]) + dot(ones, ml[...])
        for j in range(chunk_blocks):
            lanes = pl.ds(pl.multiple_of(i * chunk_blocks * LANES, LANES) + j * LANES, LANES)
            at = pl.multiple_of((i * chunk_segs + 1 + j // PER_SEG) * rows, rows)
            x[pl.ds(at, rows), pl.ds((j % PER_SEG) * LANES, LANES)] = scan(
                picked, j, weights[0, :, lanes], weights[1, :, lanes]
            )
        return carry

    lax.fori_loop(0, segs // chunk_segs, scan_chunk, 0)

    sh = tables_in[:SEG, :]
    sl = tables_in[SEG:2 * SEG, :]
    g1h, g1l = tables_in[2 * SEG:2 * SEG + HALF, :HALF], tables_in[2 * SEG:2 * SEG + HALF, HALF:]
    g2h, g2l = tables_in[2 * SEG + HALF:, :HALF], tables_in[2 * SEG + HALF:, HALF:]
    part_segs = 16
    part = part_segs * rows

    def weighted(coeffs, scale):
        return (coeffs.reshape(part_segs, rows, -1) * scale[None]).reshape(part, -1)

    def filter_part(i, carry):
        at = pl.multiple_of(i * part, part)
        middle = x[pl.ds(at + rows, part), :]
        around = 0.5 * (x[pl.ds(at, part), :] + x[pl.ds(at + 2 * rows, part), :])
        even = middle + around
        odd = middle - around
        coeffs = dot3(dot, even[:, :HALF] + even[:, HALF:], g1h, g1l)
        first = dot3(dot_t, weighted(coeffs, 0.5 * scales[:, :HALF]), g1h, g1l)
        coeffs = dot3(dot, even[:, :HALF] - even[:, HALF:], g2h, g2l)
        second = dot3(dot_t, weighted(coeffs, 0.5 * scales[:, HALF:SEG]), g2h, g2l)
        coeffs = dot3(dot, odd, sh, sl)
        third = dot3(dot_t, weighted(coeffs, scales[:, SEG:]), sh, sl)
        f[pl.ds(at, part), :HALF] = first + second + third[:, :HALF]
        f[pl.ds(at, part), HALF:] = first - second + third[:, HALF:]
        return carry

    lax.fori_loop(0, segs // part_segs, filter_part, 0)

    total[...] = jnp.zeros(total.shape, F32)

    def bin_chunk(i, carry):
        values = []
        for j in range(chunk_blocks):
            lanes = pl.ds(pl.multiple_of(i * chunk_blocks * LANES, LANES) + j * LANES, LANES)
            at = pl.multiple_of((i * chunk_segs + j // PER_SEG) * rows, rows)
            value = f[pl.ds(at, rows), pl.ds((j % PER_SEG) * LANES, LANES)]
            values.append(
                jnp.concatenate(
                    [value, weights[0, :, lanes] * value, weights[1, :, lanes] * value], axis=1
                )
            )
        vh, vl = split(jnp.concatenate(values, axis=0))
        ones = onehot[pl.ds(pl.multiple_of(i * chunk, chunk), chunk), :]
        over = (((0,), (0,)), ((), ()))
        total[...] += (
            lax.dot_general(ones, vh, over, preferred_element_type=F32)
            + lax.dot_general(ones, vl, over, preferred_element_type=F32)
        )
        return carry

    lax.fori_loop(0, segs // chunk_segs, bin_chunk, 0)
    tiles = (1, tile_sides(0)[1], tile_sides(1)[1])
    for k in range(times):
        for s in range(3):
            for g in range(groups):
                at = tiles[s] * tile_blocks + (g * times + target_of("tm", k)) * width
                out[k, s, g] = total[pl.ds(pl.multiple_of(at, 8), width), :]


def sum_kernel(arrived, parts, image, sums):
    groups = arrived.shape[0]
    rows = [jnp.zeros((1, LANES), F32)] * 4
    for j in range(groups):
        g = source_of("group", j)
        pixels = parts[0, g]
        for k in range(1, groups):
            pixels = pixels + parts[k, g]
        for c in range(3):
            a = pixels[:, c * LANES:(c + 1) * LANES]
            d = arrived[j, 0, c]
            r = arrived[j, 3, c]
            if j == 0:
                image[c] = a
            for i, term in enumerate((r * r, d * a, r * a, a * a)):
                rows[i] = rows[i] + jnp.sum(term, axis=0, keepdims=True)
    sums[...] = jnp.concatenate(rows + [jnp.zeros((4, LANES), F32)], axis=0)


def step_kernel(sums, image, arrived, solution_in, new_solution, new_residual, new_direction):
    old_norm, curvature, cross_term, image_norm = [
        jnp.sum(sums[i:i + 1, :], axis=1, keepdims=True) for i in range(4)
    ]
    step_size = old_norm / curvature
    new_norm = old_norm - 2.0 * step_size * cross_term + step_size * step_size * image_norm
    ratio = new_norm / old_norm
    for c in range(3):
        d = arrived[0, 0, c]
        residual = arrived[0, 3, c] - step_size * image[c]
        new_solution[c, 0] = solution_in[c, 0] + step_size * d
        new_residual[c, 0] = residual
        new_direction[c, 0] = residual + ratio * d


def vmem_call(kernel, out_shape, args, scratch=(), limit=24):
    spec = pl.BlockSpec(memory_space=pltpu.VMEM)
    return pl.pallas_call(
        kernel,
        out_shape=out_shape,
        in_specs=[spec] * len(args),
        out_specs=jax.tree.map(lambda _: spec, out_shape),
        scratch_shapes=list(scratch),
        compiler_params=pltpu.CompilerParams(vmem_limit_bytes=limit * 2**20),
    )(*args)


def edges(hits, stokes_int, map_residual, count):
    rows, blocks = hits.shape
    edge = jax.ShapeDtypeStruct((2 * PER_SEG + 1, rows, blocks), F32)
    spec = pl.BlockSpec(memory_space=pltpu.VMEM)
    return pl.pallas_call(
        functools.partial(edge_kernel, count),
        out_shape=[edge] * count + [jax.ShapeDtypeStruct(map_residual[:, 0].shape, F32)],
        in_specs=[spec, pl.BlockSpec(memory_space=pl.ANY), spec],
        out_specs=[spec] * (count + 1),
        scratch_shapes=[
            pltpu.VMEM((count, 2, rows, SEG), jnp.int32),
            pltpu.SemaphoreType.DMA((count,)),
        ],
        compiler_params=pltpu.CompilerParams(vmem_limit_bytes=32 * 2**20),
        cost_estimate=pl.CostEstimate(flops=0, bytes_accessed=8 * 10**6, transcendentals=0),
    )(hits, stokes_int, map_residual)


def prepare(payload, hits, stokes_int, inv_noise, depth):
    rows, samples = stokes_int.shape[1:]
    blocks = samples // LANES
    (g1h, g1l), (g2h, g2l), (sh, sl) = [np_split(table) for table in tables()]
    fixed = np.concatenate(
        [sh, sl, np.concatenate([g1h, g1l], 1), np.concatenate([g2h, g2l], 1)], axis=0
    )
    parts = 4
    out_shape = [
        jax.ShapeDtypeStruct(payload.shape, F32),
        jax.ShapeDtypeStruct(stokes_int.shape, F32),
        jax.ShapeDtypeStruct((rows * blocks, depth), BF),
        jax.ShapeDtypeStruct((rows, WIN), F32),
        jax.ShapeDtypeStruct(fixed.shape, BF),
    ]
    spec = pl.BlockSpec(memory_space=pltpu.VMEM)
    far = pl.BlockSpec(memory_space=pl.ANY)
    return pl.pallas_call(
        prep_kernel,
        out_shape=out_shape,
        in_specs=[spec, spec, spec, far, far],
        out_specs=[spec] * len(out_shape),
        scratch_shapes=[
            pltpu.VMEM((parts, 2, rows, samples // parts), jnp.int32),
            pltpu.SemaphoreType.DMA((parts + 1,)),
        ],
        compiler_params=pltpu.CompilerParams(vmem_limit_bytes=32 * 2**20),
        cost_estimate=pl.CostEstimate(flops=0, bytes_accessed=12 * 10**6, transcendentals=0),
    )(payload, hits, inv_noise, stokes_int, fixed)


def exchanged(value, axis):
    return [value] + [
        lax.ppermute(value, axis, partner_perm(axis, by)) for by in range(1, lax.axis_size(axis))
    ]


def summed(value, axis):
    count = lax.axis_size(axis)
    if count & (count - 1):
        return sum(exchanged(value, axis))
    by = 1
    while by < count:
        value = value + lax.ppermute(value, axis, partner_perm(axis, by))
        by *= 2
    return value


def shards(map_solution, map_residual, map_direction, hits, stokes_int, inv_noise):
    groups = lax.axis_size("group")
    times = lax.axis_size("tm")
    width = map_direction.shape[2]
    local = 3 * groups * times * width
    depth = -(-local // 256) * 256
    rows = hits.shape[0]
    segs = hits.shape[1] // PER_SEG

    own = map_direction[:, 0]
    near = [lax.ppermute(own, "det", tile_perm(e)) for e in range(2)]
    *edge, residual = edges(hits, stokes_int, map_residual, 1 if times == 2 else 2)
    payload = jnp.stack([own] + near + [residual])
    from_group = exchanged(payload, "group")
    payload, weights, onehot, scales, fixed = prepare(payload, hits, stokes_int, inv_noise, depth)
    arrived = jnp.stack([payload] + from_group[1:])
    if times == 2:
        sent = jnp.concatenate([arrived.reshape(-1, width, LANES), edge[0].reshape(-1, width, LANES)])
        came = lax.ppermute(sent, "tm", partner_perm("tm", 1))
        others = came[:arrived.size // (width * LANES)].reshape((1,) + arrived.shape)
        sides = [came[arrived.size // (width * LANES):].reshape(edge[0].shape)]
    else:
        forward = [(i, i + 1) for i in range(times - 1)]
        backward = [(b, a) for a, b in forward]
        sides = [lax.ppermute(edge[1], "tm", forward), lax.ppermute(edge[0], "tm", backward)]
        others = jnp.stack(exchanged(arrived, "tm")[1:])

    binned = vmem_call(
        main_kernel,
        jax.ShapeDtypeStruct((times, 3, groups, width, 3 * LANES), F32),
        [arrived, others, weights, onehot, scales, fixed] + sides,
        [
            pltpu.VMEM((depth, 3 * LANES), F32),
            pltpu.VMEM((depth, 3 * LANES), BF),
            pltpu.VMEM((depth, 3 * LANES), BF),
            pltpu.VMEM(((segs + 2) * rows, SEG), F32),
            pltpu.VMEM((segs * rows, SEG), F32),
            pltpu.VMEM((depth, 3 * LANES), F32),
        ],
    )
    half = binned[0]
    for by in range(1, times):
        half = half + lax.ppermute(binned[by], "tm", partner_perm("tm", by))
    pixels = half[0]
    for e in range(2):
        pixels = pixels + lax.ppermute(half[1 + e], "det", tile_perm(e))
    parts = jnp.stack(exchanged(pixels, "group"))
    image, sums = vmem_call(
        sum_kernel,
        [
            jax.ShapeDtypeStruct((3, width, LANES), F32),
            jax.ShapeDtypeStruct((8, LANES), F32),
        ],
        [arrived, parts],
    )
    sums = summed(summed(sums, "tm"), "det")
    return vmem_call(
        step_kernel,
        [jax.ShapeDtypeStruct(map_solution.shape, F32)] * 3,
        [sums, image, arrived, map_solution],
    )


def solution(mesh):
    map_placed = P(None, "det", ("group", "tm"), None)
    placed = (
        map_placed,
        map_placed,
        map_placed,
        P(("group", "det"), "tm"),
        P(None, ("group", "det"), "tm"),
        P(("group", "det"), None),
    )
    return jax.shard_map(
        shards,
        mesh=mesh,
        in_specs=placed,
        out_specs=(map_placed, map_placed, map_placed),
        check_vma=False,
    )
```

```python
import functools
import math

import jax
import jax.numpy as jnp
import numpy as np
from jax import lax
from jax.experimental import pallas as pl
from jax.experimental.pallas import tpu as pltpu
from jax.sharding import PartitionSpec as P

WIN = 1024
LANES = 128
SEG = WIN // 2
HALF = SEG // 2
PER_SEG = SEG // LANES
BF = jnp.bfloat16
F32 = jnp.float32


def split(value):
    high = value.astype(BF)
    return high, (value - high.astype(F32)).astype(BF)


def np_split(value):
    value = np.asarray(value, np.float32)
    high = value.astype(jnp.bfloat16)
    return high, (value - high.astype(np.float32)).astype(jnp.bfloat16)


def trig_table(samples, frequencies, length, with_ends):
    n = np.arange(samples)[:, None]
    cos_f = np.asarray(frequencies)
    sin_f = np.asarray([f for f in frequencies if not (with_ends and f in (0, length // 2))])
    angle = 2.0 * math.pi / length
    cos_t = np.cos(angle * ((n * cos_f[None, :]) % length))
    sin_t = np.sin(angle * ((n * sin_f[None, :]) % length))
    scale = np.full(len(cos_f), math.sqrt(2.0 / samples))
    if with_ends:
        scale[(cos_f == 0) | (cos_f == length // 2)] = math.sqrt(1.0 / samples)
    return np.concatenate([cos_t * scale, sin_t * math.sqrt(2.0 / samples)], axis=1)


def table_rows():
    ee = trig_table(HALF, np.arange(0, SEG + 1, 4), WIN, True)
    eo = trig_table(HALF, np.arange(2, SEG, 4), WIN, False)
    angle = 2.0 * math.pi / WIN * np.arange(HALF)
    turn = [np.tile(part(angle)[None], (16, 1)) for part in (np.cos, np.sin)]
    return np.concatenate([np.concatenate(np_split(t), axis=1) for t in (ee, eo, *turn)], axis=0)


def dot(a, b):
    return lax.dot_general(a, b, (((1,), (0,)), ((), ())), preferred_element_type=F32)


def dot_t(a, b):
    return lax.dot_general(a, b, (((1,), (1,)), ((), ())), preferred_element_type=F32)


def partner_perm(axis, by):
    count = lax.axis_size(axis)
    if count & (count - 1) == 0:
        return [(i, i ^ by) for i in range(count)]
    return [(i, (i + by) % count) for i in range(count)]


def source_of(axis, by):
    count = lax.axis_size(axis)
    me = lax.axis_index(axis)
    if count & (count - 1) == 0:
        return me ^ by
    return lax.rem(me + count - by, count)


def target_of(axis, by):
    count = lax.axis_size(axis)
    me = lax.axis_index(axis)
    if count & (count - 1) == 0:
        return me ^ by
    return lax.rem(me + by, count)


def tile_perm(exchange):
    count = lax.axis_size("det")
    if count % 2:
        return [(i, (i + 1 - 2 * exchange) % count) for i in range(count)]
    pairs = [(i, (i + 1) % count) for i in range(1 - exchange, count, 2)]
    return sorted(pairs + [(b, a) for a, b in pairs])


def tile_sides(exchange):
    if lax.axis_size("det") % 2:
        return 2 * exchange, 2 - 2 * exchange
    odd = lax.rem(lax.axis_index("det"), 2)
    side = 2 * odd if exchange == 0 else 2 - 2 * odd
    return side, side


def dot3(op, value, high, low):
    vh, vl = split(value)
    return op(vh, high) + (op(vl, high) + op(vh, low))


def edge_kernel(count, hits, stokes, residual, *refs):
    edges_out, residual_out, raw, sems = refs[:count], refs[count], refs[count + 1], refs[count + 2]
    rows, blocks = hits.shape
    samples = stokes.shape[2]
    first = [lax.axis_index("tm") == 1] if count == 1 else [True, False]
    copies = []
    for i in range(count):
        at = jnp.where(first[i], 0, samples - SEG)
        lanes = pl.ds(pl.multiple_of(at, SEG), SEG)
        copies.append(pltpu.make_async_copy(stokes.at[:, :, lanes], raw.at[i], sems.at[i]))
        copies[i].start()
    residual_out[...] = residual[:, 0]
    flags = hits[...].astype(F32) + 1.0
    last_flags = pltpu.roll(flags, PER_SEG, 1)
    for i in range(count):
        edges_out[i][2 * PER_SEG] = jnp.where(first[i], flags, last_flags)
    for i in range(count):
        copies[i].wait()
        for k in range(2):
            for j in range(PER_SEG):
                part = raw[i, k, :, j * LANES:(j + 1) * LANES]
                edges_out[i][k * PER_SEG + j] = part.astype(F32) * (1.0 / 2048.0)


def prep_kernel(
    payload, hits, inv_noise, stokes, tables_in,
    payload_out, weights, onehot, scales, tables_out, raw, sems,
):
    rows, blocks = hits.shape
    depth = onehot.shape[1]
    parts = raw.shape[0]
    width = stokes.shape[2] // parts
    copies = [
        pltpu.make_async_copy(stokes.at[:, :, pl.ds(i * width, width)], raw.at[i], sems.at[i])
        for i in range(parts)
    ]
    copies.append(pltpu.make_async_copy(tables_in, tables_out, sems.at[parts]))
    for copy in copies:
        copy.start()
    payload_out[...] = payload[...]
    ids = lax.broadcasted_iota(jnp.int32, (rows, depth), 1)
    step = 16

    def ones_of(i, carry):
        part = pltpu.roll(hits[...], blocks - i * step, 1)
        for j in range(step):
            column = jnp.broadcast_to(part[:, j:j + 1], (rows, depth))
            at = pl.multiple_of((i * step + j) * rows, rows)
            onehot[pl.ds(at, rows), :] = jnp.where(column == ids, 1.0, 0.0).astype(BF)
        return carry

    lax.fori_loop(0, blocks // step, ones_of, 0)

    freqs = inv_noise.shape[1]
    quarter = HALF // 2
    column = lax.broadcasted_iota(jnp.int32, (1, 7 * quarter), 1)
    place = lax.rem(column, quarter)
    kind = column // quarter
    wanted = 4 * place
    wanted = jnp.where(kind == 1, jnp.where(place == 0, SEG, wanted), wanted)
    wanted = jnp.where((kind == 2) | (kind == 3), wanted + 2, wanted)
    wanted = jnp.where(kind == 4, wanted + 1, wanted)
    wanted = jnp.where(kind == 5, jnp.maximum(wanted - 1, 1), wanted)
    wanted = jnp.where(kind == 6, SEG, wanted)
    wanted = jnp.broadcast_to(jnp.minimum(wanted, freqs - 1), (freqs, 7 * quarter))
    held = lax.broadcasted_iota(jnp.int32, (freqs, 7 * quarter), 0)
    chosen = jnp.where(wanted == held, 1.0, 0.0).astype(BF)
    both = dot(jnp.concatenate(split(inv_noise[...]), axis=0), chosen)
    half = 0.5 * (both[:rows] + both[rows:])
    ahead, behind, last = [half[:, i * quarter:(i + 1) * quarter] for i in (4, 5, 6)]
    mean = ahead + behind
    lane = lax.broadcasted_iota(jnp.int32, (rows, quarter), 1)
    scales[:, :SEG] = half[:, :SEG]
    scales[:, SEG:SEG + quarter] = mean
    scales[:, SEG + quarter:SEG + HALF] = jnp.where(lane == 0, 2.0 * last, mean)
    scales[:, SEG + HALF:] = ahead - behind

    for i in range(parts):
        copies[i].wait()
        for k in range(2):
            weights[k, :, pl.ds(i * width, width)] = raw[i, k].astype(F32) * (1.0 / 2048.0)
    copies[parts].wait()


def main_kernel(
    arrived, others, weights, onehot, scales, tables_in, *refs,
):
    sides, (out, window, mhl, x, f, total) = refs[:-6], refs[-6:]
    groups = lax.axis_size("group")
    times = lax.axis_size("tm")
    width = arrived.shape[3]
    rows = weights.shape[1]
    blocks = weights.shape[2] // LANES
    tile_blocks = groups * times * width
    depth = mhl.shape[0]
    local = 3 * tile_blocks
    segs = blocks // PER_SEG
    chunk_segs = 32
    chunk_blocks = chunk_segs * PER_SEG
    chunk = chunk_blocks * rows
    tiles = (1, tile_sides(1)[0], tile_sides(0)[0])

    window[...] = jnp.zeros(window.shape, F32)
    for k in range(times):
        for j in range(groups):
            at = (source_of("group", j) * times + source_of("tm", k)) * width
            for s in range(3):
                place = pl.ds(pl.multiple_of(tiles[s] * tile_blocks + at, 8), width)
                for c in range(3):
                    piece = arrived[j, s, c] if k == 0 else others[k - 1, j, s, c]
                    window[place, pl.ds(c * LANES, LANES)] = piece
    mhl[:, :3 * LANES], mhl[:, 3 * LANES:] = split(window[...])

    ids = lax.broadcasted_iota(jnp.int32, (rows, depth), 1).astype(F32)

    def scan(picked, j, q, u):
        part = picked[j * rows:(j + 1) * rows]
        return part[:, :LANES] + q * part[:, LANES:2 * LANES] + u * part[:, 2 * LANES:]

    upper_at = (segs + 1) * rows
    for at in (0, upper_at):
        x[pl.ds(at, rows), :] = jnp.zeros((rows, SEG), F32)
    if len(sides) == 1:
        places = (jnp.where(lax.axis_index("tm") == 0, upper_at, 0),)
    else:
        places = (0, upper_at)
    for side, at in zip(sides, places):
        flags = side[2 * PER_SEG] - 1.0
        ones = jnp.concatenate(
            [
                jnp.where(jnp.broadcast_to(flags[:, j:j + 1], (rows, depth)) == ids, 1.0, 0.0)
                for j in range(PER_SEG)
            ],
            axis=0,
        ).astype(BF)
        picked = dot(ones, mhl[...])
        picked = picked[:, :3 * LANES] + picked[:, 3 * LANES:]
        place = pl.ds(at if isinstance(at, int) else pl.multiple_of(at, rows), rows)
        for j in range(PER_SEG):
            x[place, pl.ds(j * LANES, LANES)] = scan(picked, j, side[j], side[PER_SEG + j])

    def scan_chunk(i, carry):
        ones = onehot[pl.ds(pl.multiple_of(i * chunk, chunk), chunk), :]
        picked = dot(ones, mhl[...])
        picked = picked[:, :3 * LANES] + picked[:, 3 * LANES:]
        for j in range(chunk_blocks):
            lanes = pl.ds(pl.multiple_of(i * chunk_blocks * LANES, LANES) + j * LANES, LANES)
            at = pl.multiple_of((i * chunk_segs + 1 + j // PER_SEG) * rows, rows)
            x[pl.ds(at, rows), pl.ds((j % PER_SEG) * LANES, LANES)] = scan(
                picked, j, weights[0, :, lanes], weights[1, :, lanes]
            )
        return carry

    lax.fori_loop(0, segs // chunk_segs, scan_chunk, 0)

    g1h, g1l = tables_in[:HALF, :HALF], tables_in[:HALF, HALF:]
    g2h, g2l = tables_in[HALF:SEG, :HALF], tables_in[HALF:SEG, HALF:]
    turn = tables_in[SEG:, :].astype(F32)
    turn = turn[:, :HALF] + turn[:, HALF:]
    cos, sin = turn[:1], turn[16:17]
    quarter = HALF // 2
    part = segs * rows

    def weighted(coeffs, at, width):
        scale = scales[:, at:at + width]
        return (coeffs.reshape(segs, rows, width) * scale[None]).reshape(part, width)

    middle = x[pl.ds(rows, part), :]
    around = 0.5 * (x[pl.ds(0, part), :] + x[pl.ds(2 * rows, part), :])
    even = middle + around
    odd = middle - around
    coeffs = dot3(dot, even[:, :HALF] - even[:, HALF:], g2h, g2l)
    second = dot3(dot_t, weighted(coeffs, HALF, HALF), g2h, g2l)
    real = cos * odd[:, :HALF] - sin * odd[:, HALF:]
    imag = sin * odd[:, :HALF] + cos * odd[:, HALF:]
    coeffs = dot3(
        dot, jnp.concatenate([even[:, :HALF] + even[:, HALF:], real, imag], axis=0), g1h, g1l
    )
    real, imag = coeffs[part:2 * part], coeffs[2 * part:]
    cross = SEG + HALF
    mixed = [
        weighted(real[:, :quarter], SEG, quarter) - weighted(imag[:, quarter:], cross, quarter),
        weighted(real[:, quarter:], SEG + quarter, quarter) + weighted(imag[:, :quarter], cross, quarter),
        weighted(imag[:, :quarter], SEG, quarter) + weighted(real[:, quarter:], cross, quarter),
        weighted(imag[:, quarter:], SEG + quarter, quarter) - weighted(real[:, :quarter], cross, quarter),
    ]
    coeffs = jnp.concatenate(
        [
            weighted(coeffs[:part], 0, HALF),
            jnp.concatenate(mixed[:2], axis=1),
            jnp.concatenate(mixed[2:], axis=1),
        ],
        axis=0,
    )
    back = dot3(dot_t, coeffs, g1h, g1l)
    first, real, imag = back[:part], back[part:2 * part], back[2 * part:]
    f[:, :HALF] = first + second + cos * real + sin * imag
    f[:, HALF:] = first - second - sin * real + cos * imag

    total[...] = jnp.zeros(total.shape, F32)

    def bin_chunk(i, carry):
        values = []
        for j in range(chunk_blocks):
            lanes = pl.ds(pl.multiple_of(i * chunk_blocks * LANES, LANES) + j * LANES, LANES)
            at = pl.multiple_of((i * chunk_segs + j // PER_SEG) * rows, rows)
            value = f[pl.ds(at, rows), pl.ds((j % PER_SEG) * LANES, LANES)]
            values.append(
                jnp.concatenate(
                    [value, weights[0, :, lanes] * value, weights[1, :, lanes] * value], axis=1
                )
            )
        ones = onehot[pl.ds(pl.multiple_of(i * chunk, chunk), chunk), :local]
        sums = lax.dot_general(
            ones,
            jnp.concatenate(split(jnp.concatenate(values, axis=0)), axis=1),
            (((0,), (0,)), ((), ())),
            preferred_element_type=F32,
        )
        total[...] += sums[:, :3 * LANES] + sums[:, 3 * LANES:]
        return carry

    lax.fori_loop(0, segs // chunk_segs, bin_chunk, 0)
    tiles = (1, tile_sides(0)[1], tile_sides(1)[1])
    for k in range(times):
        for s in range(3):
            for g in range(groups):
                at = tiles[s] * tile_blocks + (g * times + target_of("tm", k)) * width
                out[k, s, g] = total[pl.ds(pl.multiple_of(at, 8), width), :]


def sum_kernel(arrived, parts, image, sums):
    groups = arrived.shape[0]
    rows = [jnp.zeros((1, LANES), F32)] * 4
    for j in range(groups):
        g = source_of("group", j)
        pixels = parts[0, g]
        for k in range(1, groups):
            pixels = pixels + parts[k, g]
        for c in range(3):
            a = pixels[:, c * LANES:(c + 1) * LANES]
            d = arrived[j, 0, c]
            r = arrived[j, 3, c]
            if j == 0:
                image[c] = a
            for i, term in enumerate((r * r, d * a, r * a, a * a)):
                rows[i] = rows[i] + jnp.sum(term, axis=0, keepdims=True)
    sums[...] = jnp.concatenate(rows + [jnp.zeros((4, LANES), F32)], axis=0)


def step_kernel(sums, image, arrived, solution_in, new_solution, new_residual, new_direction):
    old_norm, curvature, cross_term, image_norm = [
        jnp.sum(sums[i:i + 1, :], axis=1, keepdims=True) for i in range(4)
    ]
    step_size = old_norm / curvature
    new_norm = old_norm - 2.0 * step_size * cross_term + step_size * step_size * image_norm
    ratio = new_norm / old_norm
    for c in range(3):
        d = arrived[0, 0, c]
        residual = arrived[0, 3, c] - step_size * image[c]
        new_solution[c, 0] = solution_in[c, 0] + step_size * d
        new_residual[c, 0] = residual
        new_direction[c, 0] = residual + ratio * d


def vmem_call(kernel, out_shape, args, scratch=(), limit=24):
    spec = pl.BlockSpec(memory_space=pltpu.VMEM)
    return pl.pallas_call(
        kernel,
        out_shape=out_shape,
        in_specs=[spec] * len(args),
        out_specs=jax.tree.map(lambda _: spec, out_shape),
        scratch_shapes=list(scratch),
        compiler_params=pltpu.CompilerParams(vmem_limit_bytes=limit * 2**20),
    )(*args)


def edges(hits, stokes_int, map_residual, count):
    rows, blocks = hits.shape
    edge = jax.ShapeDtypeStruct((2 * PER_SEG + 1, rows, blocks), F32)
    spec = pl.BlockSpec(memory_space=pltpu.VMEM)
    return pl.pallas_call(
        functools.partial(edge_kernel, count),
        out_shape=[edge] * count + [jax.ShapeDtypeStruct(map_residual[:, 0].shape, F32)],
        in_specs=[spec, pl.BlockSpec(memory_space=pl.ANY), spec],
        out_specs=[spec] * (count + 1),
        scratch_shapes=[
            pltpu.VMEM((count, 2, rows, SEG), jnp.int32),
            pltpu.SemaphoreType.DMA((count,)),
        ],
        compiler_params=pltpu.CompilerParams(vmem_limit_bytes=32 * 2**20),
        cost_estimate=pl.CostEstimate(flops=0, bytes_accessed=8 * 10**6, transcendentals=0),
    )(hits, stokes_int, map_residual)


def prepare(payload, hits, stokes_int, inv_noise, depth):
    rows, samples = stokes_int.shape[1:]
    blocks = samples // LANES
    fixed = table_rows()
    parts = 4
    out_shape = [
        jax.ShapeDtypeStruct(payload.shape, F32),
        jax.ShapeDtypeStruct(stokes_int.shape, F32),
        jax.ShapeDtypeStruct((rows * blocks, depth), BF),
        jax.ShapeDtypeStruct((rows, 3 * HALF + HALF // 2), F32),
        jax.ShapeDtypeStruct(fixed.shape, BF),
    ]
    spec = pl.BlockSpec(memory_space=pltpu.VMEM)
    far = pl.BlockSpec(memory_space=pl.ANY)
    return pl.pallas_call(
        prep_kernel,
        out_shape=out_shape,
        in_specs=[spec, spec, spec, far, far],
        out_specs=[spec] * len(out_shape),
        scratch_shapes=[
            pltpu.VMEM((parts, 2, rows, samples // parts), jnp.int32),
            pltpu.SemaphoreType.DMA((parts + 1,)),
        ],
        compiler_params=pltpu.CompilerParams(vmem_limit_bytes=32 * 2**20),
        cost_estimate=pl.CostEstimate(flops=0, bytes_accessed=12 * 10**6, transcendentals=0),
    )(payload, hits, inv_noise, stokes_int, fixed)


def exchanged(value, axis):
    return [value] + [
        lax.ppermute(value, axis, partner_perm(axis, by)) for by in range(1, lax.axis_size(axis))
    ]


def summed(value, axis):
    count = lax.axis_size(axis)
    if count & (count - 1):
        return sum(exchanged(value, axis))
    by = 1
    while by < count:
        value = value + lax.ppermute(value, axis, partner_perm(axis, by))
        by *= 2
    return value


def shards(map_solution, map_residual, map_direction, hits, stokes_int, inv_noise):
    groups = lax.axis_size("group")
    times = lax.axis_size("tm")
    width = map_direction.shape[2]
    local = 3 * groups * times * width
    depth = -(-local // 256) * 256
    rows = hits.shape[0]
    segs = hits.shape[1] // PER_SEG

    own = map_direction[:, 0]
    near = [lax.ppermute(own, "det", tile_perm(e)) for e in (1, 0)]
    *edge, residual = edges(hits, stokes_int, map_residual, 1 if times == 2 else 2)
    payload = jnp.stack([own] + near + [residual])
    from_group = exchanged(payload, "group")
    payload, weights, onehot, scales, fixed = prepare(payload, hits, stokes_int, inv_noise, depth)
    arrived = jnp.stack([payload] + from_group[1:])
    if times == 2:
        sent = jnp.concatenate([arrived.reshape(-1, width, LANES), edge[0].reshape(-1, width, LANES)])
        came = lax.ppermute(sent, "tm", partner_perm("tm", 1))
        others = came[:arrived.size // (width * LANES)].reshape((1,) + arrived.shape)
        sides = [came[arrived.size // (width * LANES):].reshape(edge[0].shape)]
    else:
        forward = [(i, i + 1) for i in range(times - 1)]
        backward = [(b, a) for a, b in forward]
        sides = [lax.ppermute(edge[1], "tm", forward), lax.ppermute(edge[0], "tm", backward)]
        others = jnp.stack(exchanged(arrived, "tm")[1:])

    binned = vmem_call(
        main_kernel,
        jax.ShapeDtypeStruct((times, 3, groups, width, 3 * LANES), F32),
        [arrived, others, weights, onehot, scales, fixed] + sides,
        [
            pltpu.VMEM((depth, 3 * LANES), F32),
            pltpu.VMEM((depth, 6 * LANES), BF),
            pltpu.VMEM(((segs + 2) * rows, SEG), F32),
            pltpu.VMEM((segs * rows, SEG), F32),
            pltpu.VMEM((local, 3 * LANES), F32),
        ],
    )
    half = binned[0]
    for by in range(1, times):
        half = half + lax.ppermute(binned[by], "tm", partner_perm("tm", by))
    pixels = half[0]
    for e in range(2):
        pixels = pixels + lax.ppermute(half[1 + e], "det", tile_perm(e))
    parts = jnp.stack(exchanged(pixels, "group"))
    image, sums = vmem_call(
        sum_kernel,
        [
            jax.ShapeDtypeStruct((3, width, LANES), F32),
            jax.ShapeDtypeStruct((8, LANES), F32),
        ],
        [arrived, parts],
    )
    sums = sum(exchanged(summed(sums, "tm"), "det"))
    return vmem_call(
        step_kernel,
        [jax.ShapeDtypeStruct(map_solution.shape, F32)] * 3,
        [sums, image, arrived, map_solution],
    )


def solution(mesh):
    map_placed = P(None, "det", ("group", "tm"), None)
    placed = (
        map_placed,
        map_placed,
        map_placed,
        P(("group", "det"), "tm"),
        P(None, ("group", "det"), "tm"),
        P(("group", "det"), None),
    )
    return jax.shard_map(
        shards,
        mesh=mesh,
        in_specs=placed,
        out_specs=(map_placed, map_placed, map_placed),
        check_vma=False,
    )
```

```python
import functools
import math

import jax
import jax.numpy as jnp
import numpy as np
from jax import lax
from jax.experimental import pallas as pl
from jax.experimental.pallas import tpu as pltpu
from jax.sharding import PartitionSpec as P

WIN = 1024
LANES = 128
SEG = WIN // 2
HALF = SEG // 2
PER_SEG = SEG // LANES
BF = jnp.bfloat16
F32 = jnp.float32


def split(value):
    high = value.astype(BF)
    return high, (value - high.astype(F32)).astype(BF)


def np_split(value):
    value = np.asarray(value, np.float32)
    high = value.astype(jnp.bfloat16)
    return high, (value - high.astype(np.float32)).astype(jnp.bfloat16)


def trig_table(samples, frequencies, length, with_ends):
    n = np.arange(samples)[:, None]
    cos_f = np.asarray(frequencies)
    sin_f = np.asarray([f for f in frequencies if not (with_ends and f in (0, length // 2))])
    angle = 2.0 * math.pi / length
    cos_t = np.cos(angle * ((n * cos_f[None, :]) % length))
    sin_t = np.sin(angle * ((n * sin_f[None, :]) % length))
    scale = np.full(len(cos_f), math.sqrt(2.0 / samples))
    if with_ends:
        scale[(cos_f == 0) | (cos_f == length // 2)] = math.sqrt(1.0 / samples)
    return np.concatenate([cos_t * scale, sin_t * math.sqrt(2.0 / samples)], axis=1)


def table_rows():
    ee = trig_table(HALF, np.arange(0, SEG + 1, 4), WIN, True)
    eo = trig_table(HALF, np.arange(2, SEG, 4), WIN, False)
    angle = 2.0 * math.pi / WIN * np.arange(HALF)
    turn = [np.tile(part(angle)[None], (16, 1)) for part in (np.cos, np.sin)]
    return np.concatenate([np.concatenate(np_split(t), axis=1) for t in (ee, eo, *turn)], axis=0)


def dot(a, b):
    return lax.dot_general(a, b, (((1,), (0,)), ((), ())), preferred_element_type=F32)


def dot_t(a, b):
    return lax.dot_general(a, b, (((1,), (1,)), ((), ())), preferred_element_type=F32)


def partner_perm(axis, by):
    count = lax.axis_size(axis)
    if count & (count - 1) == 0:
        return [(i, i ^ by) for i in range(count)]
    return [(i, (i + by) % count) for i in range(count)]


def source_of(axis, by):
    count = lax.axis_size(axis)
    me = lax.axis_index(axis)
    if count & (count - 1) == 0:
        return me ^ by
    return lax.rem(me + count - by, count)


def target_of(axis, by):
    count = lax.axis_size(axis)
    me = lax.axis_index(axis)
    if count & (count - 1) == 0:
        return me ^ by
    return lax.rem(me + by, count)


def tile_perm(exchange):
    count = lax.axis_size("det")
    if count % 2:
        return [(i, (i + 1 - 2 * exchange) % count) for i in range(count)]
    pairs = [(i, (i + 1) % count) for i in range(1 - exchange, count, 2)]
    return sorted(pairs + [(b, a) for a, b in pairs])


def tile_sides(exchange):
    if lax.axis_size("det") % 2:
        return 2 * exchange, 2 - 2 * exchange
    odd = lax.rem(lax.axis_index("det"), 2)
    side = 2 * odd if exchange == 0 else 2 - 2 * odd
    return side, side


def dot3(op, value, high, low):
    vh, vl = split(value)
    return op(vh, high) + (op(vl, high) + op(vh, low))


def edge_kernel(count, hits, stokes, residual, *refs):
    edges_out, residual_out, raw, sems = refs[:count], refs[count], refs[count + 1], refs[count + 2]
    rows, blocks = hits.shape
    samples = stokes.shape[2]
    first = [lax.axis_index("tm") == 1] if count == 1 else [True, False]
    copies = []
    for i in range(count):
        at = jnp.where(first[i], 0, samples - SEG)
        lanes = pl.ds(pl.multiple_of(at, SEG), SEG)
        copies.append(pltpu.make_async_copy(stokes.at[:, :, lanes], raw.at[i], sems.at[i]))
        copies[i].start()
    residual_out[...] = residual[:, 0]
    flags = hits[...].astype(F32) + 1.0
    last_flags = pltpu.roll(flags, PER_SEG, 1)
    for i in range(count):
        edges_out[i][2 * PER_SEG] = jnp.where(first[i], flags, last_flags)
    for i in range(count):
        copies[i].wait()
        for k in range(2):
            for j in range(PER_SEG):
                part = raw[i, k, :, j * LANES:(j + 1) * LANES]
                edges_out[i][k * PER_SEG + j] = part.astype(F32) * (1.0 / 2048.0)


def prep_kernel(
    payload, hits, inv_noise, stokes, tables_in,
    payload_out, weights, onehot, scales, tables_out, raw, sems,
):
    rows, blocks = hits.shape
    depth = onehot.shape[1]
    parts = raw.shape[0]
    width = stokes.shape[2] // parts
    copies = [
        pltpu.make_async_copy(stokes.at[:, :, pl.ds(i * width, width)], raw.at[i], sems.at[i])
        for i in range(parts)
    ]
    copies.append(pltpu.make_async_copy(tables_in, tables_out, sems.at[parts]))
    for copy in copies:
        copy.start()
    payload_out[...] = payload[...]
    ids = lax.broadcasted_iota(jnp.int32, (rows, depth), 1)
    step = 16

    def ones_of(i, carry):
        part = pltpu.roll(hits[...], blocks - i * step, 1)
        for j in range(step):
            column = jnp.broadcast_to(part[:, j:j + 1], (rows, depth))
            at = pl.multiple_of((i * step + j) * rows, rows)
            onehot[pl.ds(at, rows), :] = jnp.where(column == ids, 1.0, 0.0).astype(BF)
        return carry

    lax.fori_loop(0, blocks // step, ones_of, 0)

    freqs = inv_noise.shape[1]
    quarter = HALF // 2
    column = lax.broadcasted_iota(jnp.int32, (1, 7 * quarter), 1)
    place = lax.rem(column, quarter)
    kind = column // quarter
    wanted = 4 * place
    wanted = jnp.where(kind == 1, jnp.where(place == 0, SEG, wanted), wanted)
    wanted = jnp.where((kind == 2) | (kind == 3), wanted + 2, wanted)
    wanted = jnp.where(kind == 4, wanted + 1, wanted)
    wanted = jnp.where(kind == 5, jnp.maximum(wanted - 1, 1), wanted)
    wanted = jnp.where(kind == 6, SEG, wanted)
    wanted = jnp.broadcast_to(jnp.minimum(wanted, freqs - 1), (freqs, 7 * quarter))
    held = lax.broadcasted_iota(jnp.int32, (freqs, 7 * quarter), 0)
    chosen = jnp.where(wanted == held, 1.0, 0.0).astype(BF)
    both = dot(jnp.concatenate(split(inv_noise[...]), axis=0), chosen)
    half = 0.5 * (both[:rows] + both[rows:])
    ahead, behind, last = [half[:, i * quarter:(i + 1) * quarter] for i in (4, 5, 6)]
    mean = ahead + behind
    lane = lax.broadcasted_iota(jnp.int32, (rows, quarter), 1)
    scales[:, :SEG] = half[:, :SEG]
    scales[:, SEG:SEG + quarter] = mean
    scales[:, SEG + quarter:SEG + HALF] = jnp.where(lane == 0, 2.0 * last, mean)
    scales[:, SEG + HALF:] = ahead - behind

    for i in range(parts):
        copies[i].wait()
        for k in range(2):
            weights[k, :, pl.ds(i * width, width)] = raw[i, k].astype(F32) * (1.0 / 2048.0)
    copies[parts].wait()


def main_kernel(
    arrived, others, weights, onehot, scales, tables_in, *refs,
):
    sides, (out, window, mhl, x, f, total) = refs[:-6], refs[-6:]
    groups = lax.axis_size("group")
    times = lax.axis_size("tm")
    width = arrived.shape[3]
    rows = weights.shape[1]
    blocks = weights.shape[2] // LANES
    tile_blocks = groups * times * width
    depth = mhl.shape[0]
    local = 3 * tile_blocks
    segs = blocks // PER_SEG
    halves = 2
    chunk_segs = segs // halves
    chunk_blocks = chunk_segs * PER_SEG
    chunk = chunk_blocks * rows
    tiles = (1, tile_sides(1)[0], tile_sides(0)[0])

    window[...] = jnp.zeros(window.shape, F32)
    for k in range(times):
        for j in range(groups):
            at = (source_of("group", j) * times + source_of("tm", k)) * width
            for s in range(3):
                place = pl.ds(pl.multiple_of(tiles[s] * tile_blocks + at, 8), width)
                for c in range(3):
                    piece = arrived[j, s, c] if k == 0 else others[k - 1, j, s, c]
                    window[place, pl.ds(c * LANES, LANES)] = piece
    mhl[:, :3 * LANES], mhl[:, 3 * LANES:] = split(window[...])

    ids = lax.broadcasted_iota(jnp.int32, (rows, depth), 1).astype(F32)

    def scan(picked, j, q, u):
        part = picked[j * rows:(j + 1) * rows]
        return part[:, :LANES] + q * part[:, LANES:2 * LANES] + u * part[:, 2 * LANES:]

    upper_at = (segs + 1) * rows
    for at in (0, upper_at):
        x[pl.ds(at, rows), :] = jnp.zeros((rows, SEG), F32)
    if len(sides) == 1:
        places = (jnp.where(lax.axis_index("tm") == 0, upper_at, 0),)
    else:
        places = (0, upper_at)
    for side, at in zip(sides, places):
        flags = side[2 * PER_SEG] - 1.0
        ones = jnp.concatenate(
            [
                jnp.where(jnp.broadcast_to(flags[:, j:j + 1], (rows, depth)) == ids, 1.0, 0.0)
                for j in range(PER_SEG)
            ],
            axis=0,
        ).astype(BF)
        picked = dot(ones, mhl[...])
        picked = picked[:, :3 * LANES] + picked[:, 3 * LANES:]
        place = pl.ds(at if isinstance(at, int) else pl.multiple_of(at, rows), rows)
        for j in range(PER_SEG):
            x[place, pl.ds(j * LANES, LANES)] = scan(picked, j, side[j], side[PER_SEG + j])

    def scan_part(i):
        ones = onehot[i * chunk:(i + 1) * chunk, :]
        picked = dot(ones, mhl[...])
        picked = picked[:, :3 * LANES] + picked[:, 3 * LANES:]
        for j in range(chunk_blocks):
            lanes = pl.ds((i * chunk_blocks + j) * LANES, LANES)
            at = (i * chunk_segs + 1 + j // PER_SEG) * rows
            x[pl.ds(at, rows), pl.ds((j % PER_SEG) * LANES, LANES)] = scan(
                picked, j, weights[0, :, lanes], weights[1, :, lanes]
            )

    g1h, g1l = tables_in[:HALF, :HALF], tables_in[:HALF, HALF:]
    g2h, g2l = tables_in[HALF:SEG, :HALF], tables_in[HALF:SEG, HALF:]
    turn = tables_in[SEG:, :].astype(F32)
    turn = turn[:, :HALF] + turn[:, HALF:]
    cos, sin = turn[:1], turn[16:17]
    quarter = HALF // 2
    part = chunk_segs * rows

    def weighted(coeffs, at, width):
        scale = scales[:, at:at + width]
        return (coeffs.reshape(chunk_segs, rows, width) * scale[None]).reshape(part, width)

    def forward(i):
        base = i * part
        middle = x[pl.ds(base + rows, part), :]
        around = 0.5 * (x[pl.ds(base, part), :] + x[pl.ds(base + 2 * rows, part), :])
        even = middle + around
        odd = middle - around
        real = cos * odd[:, :HALF] - sin * odd[:, HALF:]
        imag = sin * odd[:, :HALF] + cos * odd[:, HALF:]
        most = jnp.concatenate([even[:, :HALF] + even[:, HALF:], real, imag], axis=0)
        return (
            dot3(dot, even[:, :HALF] - even[:, HALF:], g2h, g2l),
            dot3(dot, most, g1h, g1l),
        )

    def scaled(found):
        second, coeffs = found
        real, imag = coeffs[part:2 * part], coeffs[2 * part:]
        near, far = slice(None, quarter), slice(quarter, None)
        cross = SEG + HALF
        turned_real = [
            weighted(real[:, near], SEG, quarter) - weighted(imag[:, far], cross, quarter),
            weighted(real[:, far], SEG + quarter, quarter) + weighted(imag[:, near], cross, quarter),
        ]
        turned_imag = [
            weighted(imag[:, near], SEG, quarter) + weighted(real[:, far], cross, quarter),
            weighted(imag[:, far], SEG + quarter, quarter) - weighted(real[:, near], cross, quarter),
        ]
        most = [weighted(coeffs[:part], 0, HALF)]
        most += [jnp.concatenate(turned, axis=1) for turned in (turned_real, turned_imag)]
        return weighted(second, HALF, HALF), jnp.concatenate(most, axis=0)

    def backward(i, coeffs):
        second = dot3(dot_t, coeffs[0], g2h, g2l)
        back = dot3(dot_t, coeffs[1], g1h, g1l)
        first, real, imag = back[:part], back[part:2 * part], back[2 * part:]
        place = pl.ds(i * part, part)
        f[place, :HALF] = first + second + cos * real + sin * imag
        f[place, HALF:] = first - second - sin * real + cos * imag

    def bin_part(i):
        values = []
        for j in range(chunk_blocks):
            lanes = pl.ds((i * chunk_blocks + j) * LANES, LANES)
            at = (i * chunk_segs + j // PER_SEG) * rows
            value = f[pl.ds(at, rows), pl.ds((j % PER_SEG) * LANES, LANES)]
            values.append(
                jnp.concatenate(
                    [value, weights[0, :, lanes] * value, weights[1, :, lanes] * value], axis=1
                )
            )
        sums = lax.dot_general(
            onehot[i * chunk:(i + 1) * chunk, :local],
            jnp.concatenate(split(jnp.concatenate(values, axis=0)), axis=1),
            (((0,), (0,)), ((), ())),
            preferred_element_type=F32,
        )
        return sums[:, :3 * LANES] + sums[:, 3 * LANES:]

    scan_part(0)
    found = []
    for i in range(1, halves):
        scan_part(i)
        found.append(forward(i - 1))
    found.append(forward(halves - 1))
    sums = []
    for i in range(halves):
        backward(i, scaled(found[i]))
        if i:
            sums.append(bin_part(i - 1))
    sums.append(bin_part(halves - 1))
    total[...] = sum(sums)
    tiles = (1, tile_sides(0)[1], tile_sides(1)[1])
    for k in range(times):
        for s in range(3):
            for g in range(groups):
                at = tiles[s] * tile_blocks + (g * times + target_of("tm", k)) * width
                out[k, s, g] = total[pl.ds(pl.multiple_of(at, 8), width), :]


def sum_kernel(arrived, parts, image, sums):
    groups = arrived.shape[0]
    rows = [jnp.zeros((1, LANES), F32)] * 4
    for j in range(groups):
        g = source_of("group", j)
        pixels = parts[0, g]
        for k in range(1, groups):
            pixels = pixels + parts[k, g]
        for c in range(3):
            a = pixels[:, c * LANES:(c + 1) * LANES]
            d = arrived[j, 0, c]
            r = arrived[j, 3, c]
            if j == 0:
                image[c] = a
            for i, term in enumerate((r * r, d * a, r * a, a * a)):
                rows[i] = rows[i] + jnp.sum(term, axis=0, keepdims=True)
    sums[...] = jnp.concatenate(rows + [jnp.zeros((4, LANES), F32)], axis=0)


def step_kernel(sums, image, arrived, solution_in, new_solution, new_residual, new_direction):
    old_norm, curvature, cross_term, image_norm = [
        jnp.sum(sums[i:i + 1, :], axis=1, keepdims=True) for i in range(4)
    ]
    step_size = old_norm / curvature
    new_norm = old_norm - 2.0 * step_size * cross_term + step_size * step_size * image_norm
    ratio = new_norm / old_norm
    for c in range(3):
        d = arrived[0, 0, c]
        residual = arrived[0, 3, c] - step_size * image[c]
        new_solution[c, 0] = solution_in[c, 0] + step_size * d
        new_residual[c, 0] = residual
        new_direction[c, 0] = residual + ratio * d


def vmem_call(kernel, out_shape, args, scratch=(), limit=24):
    spec = pl.BlockSpec(memory_space=pltpu.VMEM)
    return pl.pallas_call(
        kernel,
        out_shape=out_shape,
        in_specs=[spec] * len(args),
        out_specs=jax.tree.map(lambda _: spec, out_shape),
        scratch_shapes=list(scratch),
        compiler_params=pltpu.CompilerParams(vmem_limit_bytes=limit * 2**20),
    )(*args)


def edges(hits, stokes_int, map_residual, count):
    rows, blocks = hits.shape
    edge = jax.ShapeDtypeStruct((2 * PER_SEG + 1, rows, blocks), F32)
    spec = pl.BlockSpec(memory_space=pltpu.VMEM)
    return pl.pallas_call(
        functools.partial(edge_kernel, count),
        out_shape=[edge] * count + [jax.ShapeDtypeStruct(map_residual[:, 0].shape, F32)],
        in_specs=[spec, pl.BlockSpec(memory_space=pl.ANY), spec],
        out_specs=[spec] * (count + 1),
        scratch_shapes=[
            pltpu.VMEM((count, 2, rows, SEG), jnp.int32),
            pltpu.SemaphoreType.DMA((count,)),
        ],
        compiler_params=pltpu.CompilerParams(vmem_limit_bytes=32 * 2**20),
        cost_estimate=pl.CostEstimate(flops=0, bytes_accessed=8 * 10**6, transcendentals=0),
    )(hits, stokes_int, map_residual)


def prepare(payload, hits, stokes_int, inv_noise, depth):
    rows, samples = stokes_int.shape[1:]
    blocks = samples // LANES
    fixed = table_rows()
    parts = 4
    out_shape = [
        jax.ShapeDtypeStruct(payload.shape, F32),
        jax.ShapeDtypeStruct(stokes_int.shape, F32),
        jax.ShapeDtypeStruct((rows * blocks, depth), BF),
        jax.ShapeDtypeStruct((rows, 3 * HALF + HALF // 2), F32),
        jax.ShapeDtypeStruct(fixed.shape, BF),
    ]
    spec = pl.BlockSpec(memory_space=pltpu.VMEM)
    far = pl.BlockSpec(memory_space=pl.ANY)
    return pl.pallas_call(
        prep_kernel,
        out_shape=out_shape,
        in_specs=[spec, spec, spec, far, far],
        out_specs=[spec] * len(out_shape),
        scratch_shapes=[
            pltpu.VMEM((parts, 2, rows, samples // parts), jnp.int32),
            pltpu.SemaphoreType.DMA((parts + 1,)),
        ],
        compiler_params=pltpu.CompilerParams(vmem_limit_bytes=32 * 2**20),
        cost_estimate=pl.CostEstimate(flops=0, bytes_accessed=12 * 10**6, transcendentals=0),
    )(payload, hits, inv_noise, stokes_int, fixed)


def exchanged(value, axis):
    return [value] + [
        lax.ppermute(value, axis, partner_perm(axis, by)) for by in range(1, lax.axis_size(axis))
    ]


def summed(value, axis):
    count = lax.axis_size(axis)
    if count & (count - 1):
        return sum(exchanged(value, axis))
    by = 1
    while by < count:
        value = value + lax.ppermute(value, axis, partner_perm(axis, by))
        by *= 2
    return value


def shards(map_solution, map_residual, map_direction, hits, stokes_int, inv_noise):
    groups = lax.axis_size("group")
    times = lax.axis_size("tm")
    width = map_direction.shape[2]
    local = 3 * groups * times * width
    depth = -(-local // 256) * 256
    rows = hits.shape[0]
    segs = hits.shape[1] // PER_SEG

    own = map_direction[:, 0]
    near = [lax.ppermute(own, "det", tile_perm(e)) for e in (1, 0)]
    *edge, residual = edges(hits, stokes_int, map_residual, 1 if times == 2 else 2)
    payload = jnp.stack([own] + near + [residual])
    from_group = exchanged(payload, "group")
    payload, weights, onehot, scales, fixed = prepare(payload, hits, stokes_int, inv_noise, depth)
    arrived = jnp.stack([payload] + from_group[1:])
    if times == 2:
        sent = jnp.concatenate([arrived.reshape(-1, width, LANES), edge[0].reshape(-1, width, LANES)])
        came = lax.ppermute(sent, "tm", partner_perm("tm", 1))
        others = came[:arrived.size // (width * LANES)].reshape((1,) + arrived.shape)
        sides = [came[arrived.size // (width * LANES):].reshape(edge[0].shape)]
    else:
        forward = [(i, i + 1) for i in range(times - 1)]
        backward = [(b, a) for a, b in forward]
        sides = [lax.ppermute(edge[1], "tm", forward), lax.ppermute(edge[0], "tm", backward)]
        others = jnp.stack(exchanged(arrived, "tm")[1:])

    binned = vmem_call(
        main_kernel,
        jax.ShapeDtypeStruct((times, 3, groups, width, 3 * LANES), F32),
        [arrived, others, weights, onehot, scales, fixed] + sides,
        [
            pltpu.VMEM((depth, 3 * LANES), F32),
            pltpu.VMEM((depth, 6 * LANES), BF),
            pltpu.VMEM(((segs + 2) * rows, SEG), F32),
            pltpu.VMEM((segs * rows, SEG), F32),
            pltpu.VMEM((local, 3 * LANES), F32),
        ],
    )
    half = binned[0]
    for by in range(1, times):
        half = half + lax.ppermute(binned[by], "tm", partner_perm("tm", by))
    pixels = half[0]
    for e in range(2):
        pixels = pixels + lax.ppermute(half[1 + e], "det", tile_perm(e))
    parts = jnp.stack(exchanged(pixels, "group"))
    image, sums = vmem_call(
        sum_kernel,
        [
            jax.ShapeDtypeStruct((3, width, LANES), F32),
            jax.ShapeDtypeStruct((8, LANES), F32),
        ],
        [arrived, parts],
    )
    sums = sum(exchanged(summed(sums, "tm"), "det"))
    return vmem_call(
        step_kernel,
        [jax.ShapeDtypeStruct(map_solution.shape, F32)] * 3,
        [sums, image, arrived, map_solution],
    )


def solution(mesh):
    map_placed = P(None, "det", ("group", "tm"), None)
    placed = (
        map_placed,
        map_placed,
        map_placed,
        P(("group", "det"), "tm"),
        P(None, ("group", "det"), "tm"),
        P(("group", "det"), None),
    )
    return jax.shard_map(
        shards,
        mesh=mesh,
        in_specs=placed,
        out_specs=(map_placed, map_placed, map_placed),
        check_vma=False,
    )
```

```python
import functools
import math

import jax
import jax.numpy as jnp
import numpy as np
from jax import lax
from jax.experimental import pallas as pl
from jax.experimental.pallas import tpu as pltpu
from jax.sharding import PartitionSpec as P

WIN = 1024
LANES = 128
SEG = WIN // 2
HALF = SEG // 2
PER_SEG = SEG // LANES
BF = jnp.bfloat16
F32 = jnp.float32


def split(value):
    high = value.astype(BF)
    return high, (value - high.astype(F32)).astype(BF)


def np_split(value):
    value = np.asarray(value, np.float32)
    high = value.astype(jnp.bfloat16)
    return high, (value - high.astype(np.float32)).astype(jnp.bfloat16)


def trig_table(samples, frequencies, length, with_ends):
    n = np.arange(samples)[:, None]
    cos_f = np.asarray(frequencies)
    sin_f = np.asarray([f for f in frequencies if not (with_ends and f in (0, length // 2))])
    angle = 2.0 * math.pi / length
    cos_t = np.cos(angle * ((n * cos_f[None, :]) % length))
    sin_t = np.sin(angle * ((n * sin_f[None, :]) % length))
    scale = np.full(len(cos_f), math.sqrt(2.0 / samples))
    if with_ends:
        scale[(cos_f == 0) | (cos_f == length // 2)] = math.sqrt(1.0 / samples)
    return np.concatenate([cos_t * scale, sin_t * math.sqrt(2.0 / samples)], axis=1)


def table_rows():
    ee = trig_table(HALF, np.arange(0, SEG + 1, 4), WIN, True)
    eo = trig_table(HALF, np.arange(2, SEG, 4), WIN, False)
    angle = 2.0 * math.pi / WIN * np.arange(HALF)
    turn = [np.tile(part(angle)[None], (16, 1)) for part in (np.cos, np.sin)]
    return np.concatenate([np.concatenate(np_split(t), axis=1) for t in (ee, eo, *turn)], axis=0)


def dot(a, b):
    return lax.dot_general(a, b, (((1,), (0,)), ((), ())), preferred_element_type=F32)


def dot_t(a, b):
    return lax.dot_general(a, b, (((1,), (1,)), ((), ())), preferred_element_type=F32)


def partner_perm(axis, by):
    count = lax.axis_size(axis)
    if count & (count - 1) == 0:
        return [(i, i ^ by) for i in range(count)]
    return [(i, (i + by) % count) for i in range(count)]


def source_of(axis, by):
    count = lax.axis_size(axis)
    me = lax.axis_index(axis)
    if count & (count - 1) == 0:
        return me ^ by
    return lax.rem(me + count - by, count)


def target_of(axis, by):
    count = lax.axis_size(axis)
    me = lax.axis_index(axis)
    if count & (count - 1) == 0:
        return me ^ by
    return lax.rem(me + by, count)


def tile_perm(exchange):
    count = lax.axis_size("det")
    if count % 2:
        return [(i, (i + 1 - 2 * exchange) % count) for i in range(count)]
    pairs = [(i, (i + 1) % count) for i in range(1 - exchange, count, 2)]
    return sorted(pairs + [(b, a) for a, b in pairs])


def tile_sides(exchange):
    if lax.axis_size("det") % 2:
        return 2 * exchange, 2 - 2 * exchange
    odd = lax.rem(lax.axis_index("det"), 2)
    side = 2 * odd if exchange == 0 else 2 - 2 * odd
    return side, side


def dot3(op, value, high, low):
    vh, vl = split(value)
    return op(vh, high) + (op(vl, high) + op(vh, low))


def edge_kernel(count, hits, stokes, residual, *refs):
    edges_out, residual_out, raw, sems = refs[:count], refs[count], refs[count + 1], refs[count + 2]
    rows, blocks = hits.shape
    samples = stokes.shape[2]
    first = [lax.axis_index("tm") == 1] if count == 1 else [True, False]
    copies = []
    for i in range(count):
        at = jnp.where(first[i], 0, samples - SEG)
        lanes = pl.ds(pl.multiple_of(at, SEG), SEG)
        copies.append(pltpu.make_async_copy(stokes.at[:, :, lanes], raw.at[i], sems.at[i]))
        copies[i].start()
    residual_out[...] = residual[:, 0]
    flags = hits[...].astype(F32) + 1.0
    last_flags = pltpu.roll(flags, PER_SEG, 1)
    for i in range(count):
        edges_out[i][2 * PER_SEG] = jnp.where(first[i], flags, last_flags)
    for i in range(count):
        copies[i].wait()
        for k in range(2):
            for j in range(PER_SEG):
                part = raw[i, k, :, j * LANES:(j + 1) * LANES]
                edges_out[i][k * PER_SEG + j] = part.astype(F32) * (1.0 / 2048.0)


def prep_kernel(
    payload, hits, inv_noise, stokes, tables_in,
    payload_out, weights, onehot, scales, tables_out, raw, sems,
):
    rows, blocks = hits.shape
    depth = onehot.shape[1]
    parts = raw.shape[0]
    width = stokes.shape[2] // parts
    copies = [
        pltpu.make_async_copy(stokes.at[:, :, pl.ds(i * width, width)], raw.at[i], sems.at[i])
        for i in range(parts)
    ]
    copies.append(pltpu.make_async_copy(tables_in, tables_out, sems.at[parts]))
    for copy in copies:
        copy.start()
    payload_out[...] = payload[...]
    ids = lax.broadcasted_iota(jnp.int32, (rows, depth), 1)
    step = 16

    def ones_of(i, carry):
        part = pltpu.roll(hits[...], blocks - i * step, 1)
        for j in range(step):
            column = jnp.broadcast_to(part[:, j:j + 1], (rows, depth))
            at = pl.multiple_of((i * step + j) * rows, rows)
            onehot[pl.ds(at, rows), :] = jnp.where(column == ids, 1.0, 0.0).astype(BF)
        return carry

    lax.fori_loop(0, blocks // step, ones_of, 0)

    freqs = inv_noise.shape[1]
    quarter = HALF // 2
    column = lax.broadcasted_iota(jnp.int32, (1, 7 * quarter), 1)
    place = lax.rem(column, quarter)
    kind = column // quarter
    wanted = 4 * place
    wanted = jnp.where(kind == 1, jnp.where(place == 0, SEG, wanted), wanted)
    wanted = jnp.where((kind == 2) | (kind == 3), wanted + 2, wanted)
    wanted = jnp.where(kind == 4, wanted + 1, wanted)
    wanted = jnp.where(kind == 5, jnp.maximum(wanted - 1, 1), wanted)
    wanted = jnp.where(kind == 6, SEG, wanted)
    wanted = jnp.broadcast_to(jnp.minimum(wanted, freqs - 1), (freqs, 7 * quarter))
    held = lax.broadcasted_iota(jnp.int32, (freqs, 7 * quarter), 0)
    chosen = jnp.where(wanted == held, 1.0, 0.0).astype(BF)
    both = dot(jnp.concatenate(split(inv_noise[...]), axis=0), chosen)
    half = 0.5 * (both[:rows] + both[rows:])
    ahead, behind, last = [half[:, i * quarter:(i + 1) * quarter] for i in (4, 5, 6)]
    mean = ahead + behind
    lane = lax.broadcasted_iota(jnp.int32, (rows, quarter), 1)
    scales[:, :SEG] = half[:, :SEG]
    scales[:, SEG:SEG + quarter] = mean
    scales[:, SEG + quarter:SEG + HALF] = jnp.where(lane == 0, 2.0 * last, mean)
    scales[:, SEG + HALF:] = ahead - behind

    for i in range(parts):
        copies[i].wait()
        for k in range(2):
            weights[k, :, pl.ds(i * width, width)] = raw[i, k].astype(F32) * (1.0 / 2048.0)
    copies[parts].wait()


def main_kernel(
    arrived, others, weights, onehot, scales, tables_in, *refs,
):
    sides, (out, window, mhl, x, f, total) = refs[:-6], refs[-6:]
    groups = lax.axis_size("group")
    times = lax.axis_size("tm")
    width = arrived.shape[3]
    rows = weights.shape[1]
    blocks = weights.shape[2] // LANES
    tile_blocks = groups * times * width
    depth = mhl.shape[0]
    local = 3 * tile_blocks
    segs = blocks // PER_SEG
    halves = 2
    chunk_segs = segs // halves
    chunk_blocks = chunk_segs * PER_SEG
    chunk = chunk_blocks * rows
    tiles = (1, tile_sides(1)[0], tile_sides(0)[0])

    window[...] = jnp.zeros(window.shape, F32)
    for k in range(times):
        for j in range(groups):
            at = (source_of("group", j) * times + source_of("tm", k)) * width
            for s in range(3):
                place = pl.ds(pl.multiple_of(tiles[s] * tile_blocks + at, 8), width)
                for c in range(3):
                    piece = arrived[j, s, c] if k == 0 else others[k - 1, j, s, c]
                    window[place, pl.ds(c * LANES, LANES)] = piece
    mhl[:, :3 * LANES], mhl[:, 3 * LANES:] = split(window[...])

    ids = lax.broadcasted_iota(jnp.int32, (rows, depth), 1).astype(F32)

    def scan(picked, j, q, u):
        part = picked[j * rows:(j + 1) * rows]
        return part[:, :LANES] + q * part[:, LANES:2 * LANES] + u * part[:, 2 * LANES:]

    upper_at = (segs + 1) * rows
    for at in (0, upper_at):
        x[pl.ds(at, rows), :] = jnp.zeros((rows, SEG), F32)
    if len(sides) == 1:
        places = (jnp.where(lax.axis_index("tm") == 0, upper_at, 0),)
    else:
        places = (0, upper_at)
    for side, at in zip(sides, places):
        flags = side[2 * PER_SEG] - 1.0
        ones = jnp.concatenate(
            [
                jnp.where(jnp.broadcast_to(flags[:, j:j + 1], (rows, depth)) == ids, 1.0, 0.0)
                for j in range(PER_SEG)
            ],
            axis=0,
        ).astype(BF)
        picked = dot(ones, mhl[...])
        picked = picked[:, :3 * LANES] + picked[:, 3 * LANES:]
        place = pl.ds(at if isinstance(at, int) else pl.multiple_of(at, rows), rows)
        for j in range(PER_SEG):
            x[place, pl.ds(j * LANES, LANES)] = scan(picked, j, side[j], side[PER_SEG + j])

    def scan_part(i):
        ones = onehot[i * chunk:(i + 1) * chunk, :]
        picked = dot(ones, mhl[...])
        picked = picked[:, :3 * LANES] + picked[:, 3 * LANES:]
        for j in range(chunk_blocks):
            lanes = pl.ds((i * chunk_blocks + j) * LANES, LANES)
            at = (i * chunk_segs + 1 + j // PER_SEG) * rows
            x[pl.ds(at, rows), pl.ds((j % PER_SEG) * LANES, LANES)] = scan(
                picked, j, weights[0, :, lanes], weights[1, :, lanes]
            )

    g1h, g1l = tables_in[:HALF, :HALF], tables_in[:HALF, HALF:]
    g2h, g2l = tables_in[HALF:SEG, :HALF], tables_in[HALF:SEG, HALF:]
    turn = tables_in[SEG:, :].astype(F32)
    turn = turn[:, :HALF] + turn[:, HALF:]
    cos, sin = turn[:1], turn[16:17]
    quarter = HALF // 2
    part = chunk_segs * rows

    def weighted(coeffs, at, width):
        scale = scales[:, at:at + width]
        return (coeffs.reshape(chunk_segs, rows, width) * scale[None]).reshape(part, width)

    def forward(i):
        base = i * part
        middle = x[pl.ds(base + rows, part), :]
        around = 0.5 * (x[pl.ds(base, part), :] + x[pl.ds(base + 2 * rows, part), :])
        even = middle + around
        odd = middle - around
        real = cos * odd[:, :HALF] - sin * odd[:, HALF:]
        imag = sin * odd[:, :HALF] + cos * odd[:, HALF:]
        most = jnp.concatenate([even[:, :HALF] + even[:, HALF:], real, imag], axis=0)
        return (
            dot3(dot, even[:, :HALF] - even[:, HALF:], g2h, g2l),
            dot3(dot, most, g1h, g1l),
        )

    def scaled(found):
        second, coeffs = found
        real, imag = coeffs[part:2 * part], coeffs[2 * part:]
        near, far = slice(None, quarter), slice(quarter, None)
        cross = SEG + HALF
        turned_real = [
            weighted(real[:, near], SEG, quarter) - weighted(imag[:, far], cross, quarter),
            weighted(real[:, far], SEG + quarter, quarter) + weighted(imag[:, near], cross, quarter),
        ]
        turned_imag = [
            weighted(imag[:, near], SEG, quarter) + weighted(real[:, far], cross, quarter),
            weighted(imag[:, far], SEG + quarter, quarter) - weighted(real[:, near], cross, quarter),
        ]
        most = [weighted(coeffs[:part], 0, HALF)]
        most += [jnp.concatenate(turned, axis=1) for turned in (turned_real, turned_imag)]
        return weighted(second, HALF, HALF), jnp.concatenate(most, axis=0)

    def backward(i, coeffs):
        second = dot3(dot_t, coeffs[0], g2h, g2l)
        back = dot3(dot_t, coeffs[1], g1h, g1l)
        first, real, imag = back[:part], back[part:2 * part], back[2 * part:]
        place = pl.ds(i * part, part)
        f[place, :HALF] = first + second + cos * real + sin * imag
        f[place, HALF:] = first - second - sin * real + cos * imag

    def bin_part(i):
        values = []
        for j in range(chunk_blocks):
            lanes = pl.ds((i * chunk_blocks + j) * LANES, LANES)
            at = (i * chunk_segs + j // PER_SEG) * rows
            value = f[pl.ds(at, rows), pl.ds((j % PER_SEG) * LANES, LANES)]
            values.append(
                jnp.concatenate(
                    [value, weights[0, :, lanes] * value, weights[1, :, lanes] * value], axis=1
                )
            )
        sums = lax.dot_general(
            onehot[i * chunk:(i + 1) * chunk, :local],
            jnp.concatenate(split(jnp.concatenate(values, axis=0)), axis=1),
            (((0,), (0,)), ((), ())),
            preferred_element_type=F32,
        )
        return sums[:, :3 * LANES] + sums[:, 3 * LANES:]

    scan_part(0)
    found = []
    for i in range(1, halves):
        scan_part(i)
        found.append(forward(i - 1))
    found.append(forward(halves - 1))
    sums = []
    for i in range(halves):
        backward(i, scaled(found[i]))
        if i:
            sums.append(bin_part(i - 1))
    sums.append(bin_part(halves - 1))
    total[...] = sum(sums)
    tiles = (1, tile_sides(0)[1], tile_sides(1)[1])
    for k in range(times):
        for s in range(3):
            for g in range(groups):
                at = tiles[s] * tile_blocks + (g * times + target_of("tm", k)) * width
                out[k, s, g] = total[pl.ds(pl.multiple_of(at, 8), width), :]


def sum_kernel(arrived, parts, image, sums):
    groups = arrived.shape[0]
    rows = [jnp.zeros((1, LANES), F32)] * 4
    for j in range(groups):
        g = source_of("group", j)
        pixels = parts[0, g]
        for k in range(1, groups):
            pixels = pixels + parts[k, g]
        for c in range(3):
            a = pixels[:, c * LANES:(c + 1) * LANES]
            d = arrived[j, 0, c]
            r = arrived[j, 3, c]
            if j == 0:
                image[c] = a
            for i, term in enumerate((r * r, d * a, r * a, a * a)):
                rows[i] = rows[i] + jnp.sum(term, axis=0, keepdims=True)
    sums[...] = jnp.concatenate(rows + [jnp.zeros((4, LANES), F32)], axis=0)


def step_kernel(sums, image, arrived, solution_in, new_solution, new_residual, new_direction):
    old_norm, curvature, cross_term, image_norm = [
        jnp.sum(sums[i:i + 1, :], axis=1, keepdims=True) for i in range(4)
    ]
    step_size = old_norm / curvature
    new_norm = old_norm - 2.0 * step_size * cross_term + step_size * step_size * image_norm
    ratio = new_norm / old_norm
    for c in range(3):
        d = arrived[0, 0, c]
        residual = arrived[0, 3, c] - step_size * image[c]
        new_solution[c, 0] = solution_in[c, 0] + step_size * d
        new_residual[c, 0] = residual
        new_direction[c, 0] = residual + ratio * d


def vmem_call(kernel, out_shape, args, scratch=(), limit=24):
    spec = pl.BlockSpec(memory_space=pltpu.VMEM)
    return pl.pallas_call(
        kernel,
        out_shape=out_shape,
        in_specs=[spec] * len(args),
        out_specs=jax.tree.map(lambda _: spec, out_shape),
        scratch_shapes=list(scratch),
        compiler_params=pltpu.CompilerParams(vmem_limit_bytes=limit * 2**20),
    )(*args)


def edges(hits, stokes_int, map_residual, count):
    rows, blocks = hits.shape
    edge = jax.ShapeDtypeStruct((2 * PER_SEG + 1, rows, blocks), F32)
    spec = pl.BlockSpec(memory_space=pltpu.VMEM)
    return pl.pallas_call(
        functools.partial(edge_kernel, count),
        out_shape=[edge] * count + [jax.ShapeDtypeStruct(map_residual[:, 0].shape, F32)],
        in_specs=[spec, pl.BlockSpec(memory_space=pl.ANY), spec],
        out_specs=[spec] * (count + 1),
        scratch_shapes=[
            pltpu.VMEM((count, 2, rows, SEG), jnp.int32),
            pltpu.SemaphoreType.DMA((count,)),
        ],
        compiler_params=pltpu.CompilerParams(vmem_limit_bytes=32 * 2**20),
        cost_estimate=pl.CostEstimate(flops=0, bytes_accessed=8 * 10**6, transcendentals=0),
    )(hits, stokes_int, map_residual)


def prepare(payload, hits, stokes_int, inv_noise, depth):
    rows, samples = stokes_int.shape[1:]
    blocks = samples // LANES
    fixed = table_rows()
    parts = 4
    out_shape = [
        jax.ShapeDtypeStruct(payload.shape, F32),
        jax.ShapeDtypeStruct(stokes_int.shape, F32),
        jax.ShapeDtypeStruct((rows * blocks, depth), BF),
        jax.ShapeDtypeStruct((rows, 3 * HALF + HALF // 2), F32),
        jax.ShapeDtypeStruct(fixed.shape, BF),
    ]
    spec = pl.BlockSpec(memory_space=pltpu.VMEM)
    far = pl.BlockSpec(memory_space=pl.ANY)
    return pl.pallas_call(
        prep_kernel,
        out_shape=out_shape,
        in_specs=[spec, spec, spec, far, far],
        out_specs=[spec] * len(out_shape),
        scratch_shapes=[
            pltpu.VMEM((parts, 2, rows, samples // parts), jnp.int32),
            pltpu.SemaphoreType.DMA((parts + 1,)),
        ],
        compiler_params=pltpu.CompilerParams(vmem_limit_bytes=32 * 2**20),
        cost_estimate=pl.CostEstimate(flops=0, bytes_accessed=12 * 10**6, transcendentals=0),
    )(payload, hits, inv_noise, stokes_int, fixed)


def exchanged(value, axis):
    return [value] + [
        lax.ppermute(value, axis, partner_perm(axis, by)) for by in range(1, lax.axis_size(axis))
    ]


def summed(value, axis):
    count = lax.axis_size(axis)
    if count & (count - 1):
        return sum(exchanged(value, axis))
    by = 1
    while by < count:
        value = value + lax.ppermute(value, axis, partner_perm(axis, by))
        by *= 2
    return value


def det_sum(value):
    count = lax.axis_size("det")
    if lax.axis_size("tm") != 2 or count < 4 or count & (count - 1):
        return sum(exchanged(value, "det"))
    fetched = 0.0
    for by in range(1, count // 2):
        mixed = [(2 * z + t, 2 * (z ^ (count - by if t else by)) + t) for z in range(count) for t in range(2)]
        fetched = fetched + lax.ppermute(value, ("det", "tm"), mixed)
    across = lax.ppermute(value, "det", partner_perm("det", count // 2))
    return value + across + fetched + lax.ppermute(fetched, "tm", partner_perm("tm", 1))


def shards(map_solution, map_residual, map_direction, hits, stokes_int, inv_noise):
    groups = lax.axis_size("group")
    times = lax.axis_size("tm")
    width = map_direction.shape[2]
    local = 3 * groups * times * width
    depth = -(-local // 256) * 256
    rows = hits.shape[0]
    segs = hits.shape[1] // PER_SEG

    own = map_direction[:, 0]
    near = [lax.ppermute(own, "det", tile_perm(e)) for e in (1, 0)]
    *edge, residual = edges(hits, stokes_int, map_residual, 1 if times == 2 else 2)
    payload = jnp.stack([own] + near + [residual])
    from_group = exchanged(payload, "group")
    payload, weights, onehot, scales, fixed = prepare(payload, hits, stokes_int, inv_noise, depth)
    arrived = jnp.stack([payload] + from_group[1:])
    if times == 2:
        sent = jnp.concatenate([arrived.reshape(-1, width, LANES), edge[0].reshape(-1, width, LANES)])
        came = lax.ppermute(sent, "tm", partner_perm("tm", 1))
        others = came[:arrived.size // (width * LANES)].reshape((1,) + arrived.shape)
        sides = [came[arrived.size // (width * LANES):].reshape(edge[0].shape)]
    else:
        forward = [(i, i + 1) for i in range(times - 1)]
        backward = [(b, a) for a, b in forward]
        sides = [lax.ppermute(edge[1], "tm", forward), lax.ppermute(edge[0], "tm", backward)]
        others = jnp.stack(exchanged(arrived, "tm")[1:])

    binned = vmem_call(
        main_kernel,
        jax.ShapeDtypeStruct((times, 3, groups, width, 3 * LANES), F32),
        [arrived, others, weights, onehot, scales, fixed] + sides,
        [
            pltpu.VMEM((depth, 3 * LANES), F32),
            pltpu.VMEM((depth, 6 * LANES), BF),
            pltpu.VMEM(((segs + 2) * rows, SEG), F32),
            pltpu.VMEM((segs * rows, SEG), F32),
            pltpu.VMEM((local, 3 * LANES), F32),
        ],
    )
    half = binned[0]
    for by in range(1, times):
        half = half + lax.ppermute(binned[by], "tm", partner_perm("tm", by))
    pixels = half[0]
    for e in range(2):
        pixels = pixels + lax.ppermute(half[1 + e], "det", tile_perm(e))
    parts = jnp.stack(exchanged(pixels, "group"))
    image, sums = vmem_call(
        sum_kernel,
        [
            jax.ShapeDtypeStruct((3, width, LANES), F32),
            jax.ShapeDtypeStruct((8, LANES), F32),
        ],
        [arrived, parts],
    )
    sums = det_sum(summed(sums, "tm"))
    return vmem_call(
        step_kernel,
        [jax.ShapeDtypeStruct(map_solution.shape, F32)] * 3,
        [sums, image, arrived, map_solution],
    )


def solution(mesh):
    map_placed = P(None, "det", ("group", "tm"), None)
    placed = (
        map_placed,
        map_placed,
        map_placed,
        P(("group", "det"), "tm"),
        P(None, ("group", "det"), "tm"),
        P(("group", "det"), None),
    )
    return jax.shard_map(
        shards,
        mesh=mesh,
        in_specs=placed,
        out_specs=(map_placed, map_placed, map_placed),
        check_vma=False,
    )
```

```python
import functools
import math

import jax
import jax.numpy as jnp
import numpy as np
from jax import lax
from jax.experimental import pallas as pl
from jax.experimental.pallas import tpu as pltpu
from jax.sharding import PartitionSpec as P

WIN = 1024
LANES = 128
SEG = WIN // 2
HALF = SEG // 2
PER_SEG = SEG // LANES
BF = jnp.bfloat16
F32 = jnp.float32


def split(value):
    high = value.astype(BF)
    return high, (value - high.astype(F32)).astype(BF)


def np_split(value):
    value = np.asarray(value, np.float32)
    high = value.astype(jnp.bfloat16)
    return high, (value - high.astype(np.float32)).astype(jnp.bfloat16)


def trig_table(samples, frequencies, length, with_ends):
    n = np.arange(samples)[:, None]
    cos_f = np.asarray(frequencies)
    sin_f = np.asarray([f for f in frequencies if not (with_ends and f in (0, length // 2))])
    angle = 2.0 * math.pi / length
    cos_t = np.cos(angle * ((n * cos_f[None, :]) % length))
    sin_t = np.sin(angle * ((n * sin_f[None, :]) % length))
    scale = np.full(len(cos_f), math.sqrt(2.0 / samples))
    if with_ends:
        scale[(cos_f == 0) | (cos_f == length // 2)] = math.sqrt(1.0 / samples)
    return np.concatenate([cos_t * scale, sin_t * math.sqrt(2.0 / samples)], axis=1)


def table_rows():
    ee = trig_table(HALF, np.arange(0, SEG + 1, 4), WIN, True)
    eo = trig_table(HALF, np.arange(2, SEG, 4), WIN, False)
    angle = 2.0 * math.pi / WIN * np.arange(HALF)
    turn = [np.tile(part(angle)[None], (16, 1)) for part in (np.cos, np.sin)]
    return np.concatenate([np.concatenate(np_split(t), axis=1) for t in (ee, eo, *turn)], axis=0)


def dot(a, b):
    return lax.dot_general(a, b, (((1,), (0,)), ((), ())), preferred_element_type=F32)


def dot_t(a, b):
    return lax.dot_general(a, b, (((1,), (1,)), ((), ())), preferred_element_type=F32)


def partner_perm(axis, by):
    count = lax.axis_size(axis)
    if count & (count - 1) == 0:
        return [(i, i ^ by) for i in range(count)]
    return [(i, (i + by) % count) for i in range(count)]


def source_of(axis, by):
    count = lax.axis_size(axis)
    me = lax.axis_index(axis)
    if count & (count - 1) == 0:
        return me ^ by
    return lax.rem(me + count - by, count)


def target_of(axis, by):
    count = lax.axis_size(axis)
    me = lax.axis_index(axis)
    if count & (count - 1) == 0:
        return me ^ by
    return lax.rem(me + by, count)


def tile_perm(exchange):
    count = lax.axis_size("det")
    if count % 2:
        return [(i, (i + 1 - 2 * exchange) % count) for i in range(count)]
    pairs = [(i, (i + 1) % count) for i in range(1 - exchange, count, 2)]
    return sorted(pairs + [(b, a) for a, b in pairs])


def tile_sides(exchange):
    if lax.axis_size("det") % 2:
        return 2 * exchange, 2 - 2 * exchange
    odd = lax.rem(lax.axis_index("det"), 2)
    side = 2 * odd if exchange == 0 else 2 - 2 * odd
    return side, side


def dot3(op, value, high, low):
    vh, vl = split(value)
    return op(vh, high) + (op(vl, high) + op(vh, low))


def edge_kernel(count, hits, stokes, residual, *refs):
    edges_out, residual_out, raw, sems = refs[:count], refs[count], refs[count + 1], refs[count + 2]
    rows, blocks = hits.shape
    samples = stokes.shape[2]
    first = [lax.axis_index("tm") == 1] if count == 1 else [True, False]
    copies = []
    for i in range(count):
        at = jnp.where(first[i], 0, samples - SEG)
        lanes = pl.ds(pl.multiple_of(at, SEG), SEG)
        copies.append(pltpu.make_async_copy(stokes.at[:, :, lanes], raw.at[i], sems.at[i]))
        copies[i].start()
    residual_out[...] = residual[:, 0]
    flags = hits[...].astype(F32) + 1.0
    last_flags = pltpu.roll(flags, PER_SEG, 1)
    for i in range(count):
        edges_out[i][2 * PER_SEG] = jnp.where(first[i], flags, last_flags)
    for i in range(count):
        copies[i].wait()
        for k in range(2):
            for j in range(PER_SEG):
                part = raw[i, k, :, j * LANES:(j + 1) * LANES]
                edges_out[i][k * PER_SEG + j] = part.astype(F32) * (1.0 / 2048.0)


def prep_kernel(
    payload, hits, inv_noise, stokes, tables_in,
    payload_out, weights, onehot, scales, tables_out, raw, sems,
):
    rows, blocks = hits.shape
    depth = onehot.shape[1]
    parts = raw.shape[0]
    width = stokes.shape[2] // parts
    copies = [
        pltpu.make_async_copy(stokes.at[:, :, pl.ds(i * width, width)], raw.at[i], sems.at[i])
        for i in range(parts)
    ]
    copies.append(pltpu.make_async_copy(tables_in, tables_out, sems.at[parts]))
    for copy in copies:
        copy.start()
    payload_out[...] = payload[...]
    ids = lax.broadcasted_iota(jnp.int32, (rows, depth), 1)
    step = 16

    def ones_of(i, carry):
        part = pltpu.roll(hits[...], blocks - i * step, 1)
        for j in range(step):
            column = jnp.broadcast_to(part[:, j:j + 1], (rows, depth))
            at = pl.multiple_of((i * step + j) * rows, rows)
            onehot[pl.ds(at, rows), :] = jnp.where(column == ids, 1.0, 0.0).astype(BF)
        return carry

    lax.fori_loop(0, blocks // step, ones_of, 0)

    freqs = inv_noise.shape[1]
    quarter = HALF // 2
    column = lax.broadcasted_iota(jnp.int32, (1, 7 * quarter), 1)
    place = lax.rem(column, quarter)
    kind = column // quarter
    wanted = 4 * place
    wanted = jnp.where(kind == 1, jnp.where(place == 0, SEG, wanted), wanted)
    wanted = jnp.where((kind == 2) | (kind == 3), wanted + 2, wanted)
    wanted = jnp.where(kind == 4, wanted + 1, wanted)
    wanted = jnp.where(kind == 5, jnp.maximum(wanted - 1, 1), wanted)
    wanted = jnp.where(kind == 6, SEG, wanted)
    wanted = jnp.broadcast_to(jnp.minimum(wanted, freqs - 1), (freqs, 7 * quarter))
    held = lax.broadcasted_iota(jnp.int32, (freqs, 7 * quarter), 0)
    chosen = jnp.where(wanted == held, 1.0, 0.0).astype(BF)
    both = dot(jnp.concatenate(split(inv_noise[...]), axis=0), chosen)
    half = 0.5 * (both[:rows] + both[rows:])
    ahead, behind, last = [half[:, i * quarter:(i + 1) * quarter] for i in (4, 5, 6)]
    mean = ahead + behind
    lane = lax.broadcasted_iota(jnp.int32, (rows, quarter), 1)
    scales[:, :SEG] = half[:, :SEG]
    scales[:, SEG:SEG + quarter] = mean
    scales[:, SEG + quarter:SEG + HALF] = jnp.where(lane == 0, 2.0 * last, mean)
    scales[:, SEG + HALF:] = ahead - behind

    for i in range(parts):
        copies[i].wait()
        for k in range(2):
            weights[k, :, pl.ds(i * width, width)] = raw[i, k].astype(F32) * (1.0 / 2048.0)
    copies[parts].wait()


def main_kernel(
    arrived, others, weights, onehot, scales, tables_in, *refs,
):
    sides, (out, window, mhl, x, f, total) = refs[:-6], refs[-6:]
    groups = lax.axis_size("group")
    times = lax.axis_size("tm")
    width = arrived.shape[3]
    rows = weights.shape[1]
    blocks = weights.shape[2] // LANES
    tile_blocks = groups * times * width
    depth = mhl.shape[0]
    local = 3 * tile_blocks
    segs = blocks // PER_SEG
    halves = 2
    chunk_segs = segs // halves
    chunk_blocks = chunk_segs * PER_SEG
    chunk = chunk_blocks * rows
    tiles = (1, tile_sides(1)[0], tile_sides(0)[0])

    window[...] = jnp.zeros(window.shape, F32)
    for k in range(times):
        core = source_of("tm", k)
        if times == 2:
            near = jnp.where(core == 0, tile_sides(1)[0], tile_sides(0)[0])
            spots = [(1, core), (near, core), (near, 1 - core)]
        else:
            spots = [(tile, core) for tile in tiles]
        for j in range(groups):
            for s, (tile, share) in enumerate(spots):
                at = tile * tile_blocks + (source_of("group", j) * times + share) * width
                place = pl.ds(pl.multiple_of(at, 8), width)
                for c in range(3):
                    piece = arrived[j, s, c] if k == 0 else others[k - 1, j, s, c]
                    window[place, pl.ds(c * LANES, LANES)] = piece
    mhl[:, :3 * LANES], mhl[:, 3 * LANES:] = split(window[...])

    ids = lax.broadcasted_iota(jnp.int32, (rows, depth), 1).astype(F32)

    def scan(picked, j, q, u):
        part = picked[j * rows:(j + 1) * rows]
        return part[:, :LANES] + q * part[:, LANES:2 * LANES] + u * part[:, 2 * LANES:]

    upper_at = (segs + 1) * rows
    for at in (0, upper_at):
        x[pl.ds(at, rows), :] = jnp.zeros((rows, SEG), F32)
    if len(sides) == 1:
        places = (jnp.where(lax.axis_index("tm") == 0, upper_at, 0),)
    else:
        places = (0, upper_at)
    for side, at in zip(sides, places):
        flags = side[2 * PER_SEG] - 1.0
        ones = jnp.concatenate(
            [
                jnp.where(jnp.broadcast_to(flags[:, j:j + 1], (rows, depth)) == ids, 1.0, 0.0)
                for j in range(PER_SEG)
            ],
            axis=0,
        ).astype(BF)
        picked = dot(ones, mhl[...])
        picked = picked[:, :3 * LANES] + picked[:, 3 * LANES:]
        place = pl.ds(at if isinstance(at, int) else pl.multiple_of(at, rows), rows)
        for j in range(PER_SEG):
            x[place, pl.ds(j * LANES, LANES)] = scan(picked, j, side[j], side[PER_SEG + j])

    def scan_part(i):
        ones = onehot[i * chunk:(i + 1) * chunk, :]
        picked = dot(ones, mhl[...])
        picked = picked[:, :3 * LANES] + picked[:, 3 * LANES:]
        for j in range(chunk_blocks):
            lanes = pl.ds((i * chunk_blocks + j) * LANES, LANES)
            at = (i * chunk_segs + 1 + j // PER_SEG) * rows
            x[pl.ds(at, rows), pl.ds((j % PER_SEG) * LANES, LANES)] = scan(
                picked, j, weights[0, :, lanes], weights[1, :, lanes]
            )

    g1h, g1l = tables_in[:HALF, :HALF], tables_in[:HALF, HALF:]
    g2h, g2l = tables_in[HALF:SEG, :HALF], tables_in[HALF:SEG, HALF:]
    turn = tables_in[SEG:, :].astype(F32)
    turn = turn[:, :HALF] + turn[:, HALF:]
    cos, sin = turn[:1], turn[16:17]
    quarter = HALF // 2
    part = chunk_segs * rows

    def weighted(coeffs, at, width):
        scale = scales[:, at:at + width]
        return (coeffs.reshape(chunk_segs, rows, width) * scale[None]).reshape(part, width)

    def forward(i):
        base = i * part
        middle = x[pl.ds(base + rows, part), :]
        around = 0.5 * (x[pl.ds(base, part), :] + x[pl.ds(base + 2 * rows, part), :])
        even = middle + around
        odd = middle - around
        real = cos * odd[:, :HALF] - sin * odd[:, HALF:]
        imag = sin * odd[:, :HALF] + cos * odd[:, HALF:]
        most = jnp.concatenate([even[:, :HALF] + even[:, HALF:], real, imag], axis=0)
        return (
            dot3(dot, even[:, :HALF] - even[:, HALF:], g2h, g2l),
            dot3(dot, most, g1h, g1l),
        )

    def scaled(found):
        second, coeffs = found
        real, imag = coeffs[part:2 * part], coeffs[2 * part:]
        near, far = slice(None, quarter), slice(quarter, None)
        cross = SEG + HALF
        turned_real = [
            weighted(real[:, near], SEG, quarter) - weighted(imag[:, far], cross, quarter),
            weighted(real[:, far], SEG + quarter, quarter) + weighted(imag[:, near], cross, quarter),
        ]
        turned_imag = [
            weighted(imag[:, near], SEG, quarter) + weighted(real[:, far], cross, quarter),
            weighted(imag[:, far], SEG + quarter, quarter) - weighted(real[:, near], cross, quarter),
        ]
        most = [weighted(coeffs[:part], 0, HALF)]
        most += [jnp.concatenate(turned, axis=1) for turned in (turned_real, turned_imag)]
        return weighted(second, HALF, HALF), jnp.concatenate(most, axis=0)

    def backward(i, coeffs):
        second = dot3(dot_t, coeffs[0], g2h, g2l)
        back = dot3(dot_t, coeffs[1], g1h, g1l)
        first, real, imag = back[:part], back[part:2 * part], back[2 * part:]
        place = pl.ds(i * part, part)
        f[place, :HALF] = first + second + cos * real + sin * imag
        f[place, HALF:] = first - second - sin * real + cos * imag

    def bin_part(i):
        values = []
        for j in range(chunk_blocks):
            lanes = pl.ds((i * chunk_blocks + j) * LANES, LANES)
            at = (i * chunk_segs + j // PER_SEG) * rows
            value = f[pl.ds(at, rows), pl.ds((j % PER_SEG) * LANES, LANES)]
            values.append(
                jnp.concatenate(
                    [value, weights[0, :, lanes] * value, weights[1, :, lanes] * value], axis=1
                )
            )
        sums = lax.dot_general(
            onehot[i * chunk:(i + 1) * chunk, :local],
            jnp.concatenate(split(jnp.concatenate(values, axis=0)), axis=1),
            (((0,), (0,)), ((), ())),
            preferred_element_type=F32,
        )
        return sums[:, :3 * LANES] + sums[:, 3 * LANES:]

    scan_part(0)
    found = []
    for i in range(1, halves):
        scan_part(i)
        found.append(forward(i - 1))
    found.append(forward(halves - 1))
    sums = []
    for i in range(halves):
        backward(i, scaled(found[i]))
        if i:
            sums.append(bin_part(i - 1))
    sums.append(bin_part(halves - 1))
    total[...] = sum(sums)
    tiles = (1, tile_sides(0)[1], tile_sides(1)[1])
    for k in range(times):
        for s in range(3):
            for g in range(groups):
                at = tiles[s] * tile_blocks + (g * times + target_of("tm", k)) * width
                out[k, s, g] = total[pl.ds(pl.multiple_of(at, 8), width), :]


def sum_kernel(arrived, parts, image, sums):
    groups = arrived.shape[0]
    rows = [jnp.zeros((1, LANES), F32)] * 4
    for j in range(groups):
        g = source_of("group", j)
        pixels = parts[0, g]
        for k in range(1, groups):
            pixels = pixels + parts[k, g]
        for c in range(3):
            a = pixels[:, c * LANES:(c + 1) * LANES]
            d = arrived[j, 0, c]
            r = arrived[j, 3, c]
            if j == 0:
                image[c] = a
            for i, term in enumerate((r * r, d * a, r * a, a * a)):
                rows[i] = rows[i] + jnp.sum(term, axis=0, keepdims=True)
    sums[...] = jnp.concatenate(rows + [jnp.zeros((4, LANES), F32)], axis=0)


def step_kernel(sums, image, arrived, solution_in, new_solution, new_residual, new_direction):
    old_norm, curvature, cross_term, image_norm = [
        jnp.sum(sums[i:i + 1, :], axis=1, keepdims=True) for i in range(4)
    ]
    step_size = old_norm / curvature
    new_norm = old_norm - 2.0 * step_size * cross_term + step_size * step_size * image_norm
    ratio = new_norm / old_norm
    for c in range(3):
        d = arrived[0, 0, c]
        residual = arrived[0, 3, c] - step_size * image[c]
        new_solution[c, 0] = solution_in[c, 0] + step_size * d
        new_residual[c, 0] = residual
        new_direction[c, 0] = residual + ratio * d


def copy_kernel(source, target):
    target[...] = source[:, 0]


def vmem_call(kernel, out_shape, args, scratch=(), limit=24):
    spec = pl.BlockSpec(memory_space=pltpu.VMEM)
    return pl.pallas_call(
        kernel,
        out_shape=out_shape,
        in_specs=[spec] * len(args),
        out_specs=jax.tree.map(lambda _: spec, out_shape),
        scratch_shapes=list(scratch),
        compiler_params=pltpu.CompilerParams(vmem_limit_bytes=limit * 2**20),
    )(*args)


def edges(hits, stokes_int, map_residual, count):
    rows, blocks = hits.shape
    edge = jax.ShapeDtypeStruct((2 * PER_SEG + 1, rows, blocks), F32)
    spec = pl.BlockSpec(memory_space=pltpu.VMEM)
    return pl.pallas_call(
        functools.partial(edge_kernel, count),
        out_shape=[edge] * count + [jax.ShapeDtypeStruct(map_residual[:, 0].shape, F32)],
        in_specs=[spec, pl.BlockSpec(memory_space=pl.ANY), spec],
        out_specs=[spec] * (count + 1),
        scratch_shapes=[
            pltpu.VMEM((count, 2, rows, SEG), jnp.int32),
            pltpu.SemaphoreType.DMA((count,)),
        ],
        compiler_params=pltpu.CompilerParams(vmem_limit_bytes=32 * 2**20),
        cost_estimate=pl.CostEstimate(flops=0, bytes_accessed=8 * 10**6, transcendentals=0),
    )(hits, stokes_int, map_residual)


def prepare(payload, hits, stokes_int, inv_noise, depth):
    rows, samples = stokes_int.shape[1:]
    blocks = samples // LANES
    fixed = table_rows()
    parts = 4
    out_shape = [
        jax.ShapeDtypeStruct(payload.shape, F32),
        jax.ShapeDtypeStruct(stokes_int.shape, F32),
        jax.ShapeDtypeStruct((rows * blocks, depth), BF),
        jax.ShapeDtypeStruct((rows, 3 * HALF + HALF // 2), F32),
        jax.ShapeDtypeStruct(fixed.shape, BF),
    ]
    spec = pl.BlockSpec(memory_space=pltpu.VMEM)
    far = pl.BlockSpec(memory_space=pl.ANY)
    return pl.pallas_call(
        prep_kernel,
        out_shape=out_shape,
        in_specs=[spec, spec, spec, far, far],
        out_specs=[spec] * len(out_shape),
        scratch_shapes=[
            pltpu.VMEM((parts, 2, rows, samples // parts), jnp.int32),
            pltpu.SemaphoreType.DMA((parts + 1,)),
        ],
        compiler_params=pltpu.CompilerParams(vmem_limit_bytes=32 * 2**20),
        cost_estimate=pl.CostEstimate(flops=0, bytes_accessed=12 * 10**6, transcendentals=0),
    )(payload, hits, inv_noise, stokes_int, fixed)


def exchanged(value, axis):
    return [value] + [
        lax.ppermute(value, axis, partner_perm(axis, by)) for by in range(1, lax.axis_size(axis))
    ]


def summed(value, axis):
    count = lax.axis_size(axis)
    if count & (count - 1):
        return sum(exchanged(value, axis))
    by = 1
    while by < count:
        value = value + lax.ppermute(value, axis, partner_perm(axis, by))
        by *= 2
    return value


def det_sum(value):
    count = lax.axis_size("det")
    if lax.axis_size("tm") != 2 or count < 4 or count & (count - 1):
        return sum(exchanged(value, "det"))
    fetched = 0.0
    for by in range(1, count // 2):
        mixed = [(2 * z + t, 2 * (z ^ (count - by if t else by)) + t) for z in range(count) for t in range(2)]
        fetched = fetched + lax.ppermute(value, ("det", "tm"), mixed)
    across = lax.ppermute(value, "det", partner_perm("det", count // 2))
    return value + across + fetched + lax.ppermute(fetched, "tm", partner_perm("tm", 1))


def shards(map_solution, map_residual, map_direction, hits, stokes_int, inv_noise):
    groups = lax.axis_size("group")
    times = lax.axis_size("tm")
    width = map_direction.shape[2]
    local = 3 * groups * times * width
    depth = -(-local // 256) * 256
    rows = hits.shape[0]
    segs = hits.shape[1] // PER_SEG

    own = map_direction[:, 0]
    if times == 2:
        mixed = [(2 * a + t, 2 * b + t) for t in range(2) for a, b in tile_perm(1 - t)]
        other = lax.ppermute(own, "tm", partner_perm("tm", 1))
        own = vmem_call(copy_kernel, jax.ShapeDtypeStruct(own.shape, F32), [map_direction])
        pair = jnp.stack([own, other])
        near = list(lax.ppermute(pair, ("det", "tm"), mixed))
    else:
        near = [lax.ppermute(own, "det", tile_perm(e)) for e in (1, 0)]
    *edge, residual = edges(hits, stokes_int, map_residual, 1 if times == 2 else 2)
    payload = jnp.stack([own] + near + [residual])
    from_group = exchanged(payload, "group")
    payload, weights, onehot, scales, fixed = prepare(payload, hits, stokes_int, inv_noise, depth)
    arrived = jnp.stack([payload] + from_group[1:])
    if times == 2:
        sent = jnp.concatenate([arrived.reshape(-1, width, LANES), edge[0].reshape(-1, width, LANES)])
        came = lax.ppermute(sent, "tm", partner_perm("tm", 1))
        others = came[:arrived.size // (width * LANES)].reshape((1,) + arrived.shape)
        sides = [came[arrived.size // (width * LANES):].reshape(edge[0].shape)]
    else:
        forward = [(i, i + 1) for i in range(times - 1)]
        backward = [(b, a) for a, b in forward]
        sides = [lax.ppermute(edge[1], "tm", forward), lax.ppermute(edge[0], "tm", backward)]
        others = jnp.stack(exchanged(arrived, "tm")[1:])

    binned = vmem_call(
        main_kernel,
        jax.ShapeDtypeStruct((times, 3, groups, width, 3 * LANES), F32),
        [arrived, others, weights, onehot, scales, fixed] + sides,
        [
            pltpu.VMEM((depth, 3 * LANES), F32),
            pltpu.VMEM((depth, 6 * LANES), BF),
            pltpu.VMEM(((segs + 2) * rows, SEG), F32),
            pltpu.VMEM((segs * rows, SEG), F32),
            pltpu.VMEM((local, 3 * LANES), F32),
        ],
    )
    half = binned[0]
    for by in range(1, times):
        half = half + lax.ppermute(binned[by], "tm", partner_perm("tm", by))
    pixels = half[0]
    for e in range(2):
        pixels = pixels + lax.ppermute(half[1 + e], "det", tile_perm(e))
    parts = jnp.stack(exchanged(pixels, "group"))
    image, sums = vmem_call(
        sum_kernel,
        [
            jax.ShapeDtypeStruct((3, width, LANES), F32),
            jax.ShapeDtypeStruct((8, LANES), F32),
        ],
        [arrived, parts],
    )
    sums = det_sum(summed(sums, "tm"))
    return vmem_call(
        step_kernel,
        [jax.ShapeDtypeStruct(map_solution.shape, F32)] * 3,
        [sums, image, arrived, map_solution],
    )


def solution(mesh):
    map_placed = P(None, "det", ("group", "tm"), None)
    placed = (
        map_placed,
        map_placed,
        map_placed,
        P(("group", "det"), "tm"),
        P(None, ("group", "det"), "tm"),
        P(("group", "det"), None),
    )
    return jax.shard_map(
        shards,
        mesh=mesh,
        in_specs=placed,
        out_specs=(map_placed, map_placed, map_placed),
        check_vma=False,
    )
```

```python
import functools
import math

import jax
import jax.numpy as jnp
import numpy as np
from jax import lax
from jax.experimental import pallas as pl
from jax.experimental.pallas import tpu as pltpu
from jax.sharding import PartitionSpec as P

WIN = 1024
LANES = 128
SEG = WIN // 2
HALF = SEG // 2
PER_SEG = SEG // LANES
BF = jnp.bfloat16
F32 = jnp.float32


def split(value):
    high = value.astype(BF)
    return high, (value - high.astype(F32)).astype(BF)


def np_split(value):
    value = np.asarray(value, np.float32)
    high = value.astype(jnp.bfloat16)
    return high, (value - high.astype(np.float32)).astype(jnp.bfloat16)


def trig_table(samples, frequencies, length, with_ends):
    n = np.arange(samples)[:, None]
    cos_f = np.asarray(frequencies)
    sin_f = np.asarray([f for f in frequencies if not (with_ends and f in (0, length // 2))])
    angle = 2.0 * math.pi / length
    cos_t = np.cos(angle * ((n * cos_f[None, :]) % length))
    sin_t = np.sin(angle * ((n * sin_f[None, :]) % length))
    scale = np.full(len(cos_f), math.sqrt(2.0 / samples))
    if with_ends:
        scale[(cos_f == 0) | (cos_f == length // 2)] = math.sqrt(1.0 / samples)
    return np.concatenate([cos_t * scale, sin_t * math.sqrt(2.0 / samples)], axis=1)


def table_rows():
    ee = trig_table(HALF, np.arange(0, SEG + 1, 4), WIN, True)
    eo = trig_table(HALF, np.arange(2, SEG, 4), WIN, False)
    angle = 2.0 * math.pi / WIN * np.arange(HALF)
    turn = [np.tile(part(angle)[None], (16, 1)) for part in (np.cos, np.sin)]
    return np.concatenate([np.concatenate(np_split(t), axis=1) for t in (ee, eo, *turn)], axis=0)


def dot(a, b):
    return lax.dot_general(a, b, (((1,), (0,)), ((), ())), preferred_element_type=F32)


def dot_t(a, b):
    return lax.dot_general(a, b, (((1,), (1,)), ((), ())), preferred_element_type=F32)


def partner_perm(axis, by):
    count = lax.axis_size(axis)
    if count & (count - 1) == 0:
        return [(i, i ^ by) for i in range(count)]
    return [(i, (i + by) % count) for i in range(count)]


def source_of(axis, by):
    count = lax.axis_size(axis)
    me = lax.axis_index(axis)
    if count & (count - 1) == 0:
        return me ^ by
    return lax.rem(me + count - by, count)


def target_of(axis, by):
    count = lax.axis_size(axis)
    me = lax.axis_index(axis)
    if count & (count - 1) == 0:
        return me ^ by
    return lax.rem(me + by, count)


def tile_perm(exchange):
    count = lax.axis_size("det")
    if count % 2:
        return [(i, (i + 1 - 2 * exchange) % count) for i in range(count)]
    pairs = [(i, (i + 1) % count) for i in range(1 - exchange, count, 2)]
    return sorted(pairs + [(b, a) for a, b in pairs])


def tile_sides(exchange):
    if lax.axis_size("det") % 2:
        return 2 * exchange, 2 - 2 * exchange
    odd = lax.rem(lax.axis_index("det"), 2)
    side = 2 * odd if exchange == 0 else 2 - 2 * odd
    return side, side


def dot3(op, value, high, low):
    vh, vl = split(value)
    axis = 0 if op is dot else 1
    small = jnp.concatenate([high, low], axis=axis)
    return op(vh, high) + op(jnp.concatenate([vl, vh], axis=1), small)


def edge_kernel(count, hits, stokes, residual, *refs):
    edges_out, residual_out, raw, sems = refs[:count], refs[count], refs[count + 1], refs[count + 2]
    rows, blocks = hits.shape
    samples = stokes.shape[2]
    first = [lax.axis_index("tm") == 1] if count == 1 else [True, False]
    copies = []
    for i in range(count):
        at = jnp.where(first[i], 0, samples - SEG)
        lanes = pl.ds(pl.multiple_of(at, SEG), SEG)
        copies.append(pltpu.make_async_copy(stokes.at[:, :, lanes], raw.at[i], sems.at[i]))
        copies[i].start()
    residual_out[...] = residual[:, 0]
    flags = hits[...].astype(F32) + 1.0
    last_flags = pltpu.roll(flags, PER_SEG, 1)
    for i in range(count):
        edges_out[i][2 * PER_SEG] = jnp.where(first[i], flags, last_flags)
    for i in range(count):
        copies[i].wait()
        for k in range(2):
            for j in range(PER_SEG):
                part = raw[i, k, :, j * LANES:(j + 1) * LANES]
                edges_out[i][k * PER_SEG + j] = part.astype(F32) * (1.0 / 2048.0)


def prep_kernel(
    payload, hits, inv_noise, stokes, tables_in,
    payload_out, weights, onehot, scales, tables_out, raw, sems,
):
    rows, blocks = hits.shape
    depth = onehot.shape[1]
    parts = raw.shape[0]
    width = stokes.shape[2] // parts
    copies = [
        pltpu.make_async_copy(stokes.at[:, :, pl.ds(i * width, width)], raw.at[i], sems.at[i])
        for i in range(parts)
    ]
    copies.append(pltpu.make_async_copy(tables_in, tables_out, sems.at[parts]))
    for copy in copies:
        copy.start()
    payload_out[...] = payload[...]
    ids = lax.broadcasted_iota(jnp.int32, (rows, depth), 1)
    step = 16

    def ones_of(i, carry):
        part = pltpu.roll(hits[...], blocks - i * step, 1)
        for j in range(step):
            column = jnp.broadcast_to(part[:, j:j + 1], (rows, depth))
            at = pl.multiple_of((i * step + j) * rows, rows)
            onehot[pl.ds(at, rows), :] = jnp.where(column == ids, 1.0, 0.0).astype(BF)
        return carry

    lax.fori_loop(0, blocks // step, ones_of, 0)

    freqs = inv_noise.shape[1]
    quarter = HALF // 2
    column = lax.broadcasted_iota(jnp.int32, (1, 7 * quarter), 1)
    place = lax.rem(column, quarter)
    kind = column // quarter
    wanted = 4 * place
    wanted = jnp.where(kind == 1, jnp.where(place == 0, SEG, wanted), wanted)
    wanted = jnp.where((kind == 2) | (kind == 3), wanted + 2, wanted)
    wanted = jnp.where(kind == 4, wanted + 1, wanted)
    wanted = jnp.where(kind == 5, jnp.maximum(wanted - 1, 1), wanted)
    wanted = jnp.where(kind == 6, SEG, wanted)
    wanted = jnp.broadcast_to(jnp.minimum(wanted, freqs - 1), (freqs, 7 * quarter))
    held = lax.broadcasted_iota(jnp.int32, (freqs, 7 * quarter), 0)
    chosen = jnp.where(wanted == held, 1.0, 0.0).astype(BF)
    both = dot(jnp.concatenate(split(inv_noise[...]), axis=0), chosen)
    half = 0.5 * (both[:rows] + both[rows:])
    ahead, behind, last = [half[:, i * quarter:(i + 1) * quarter] for i in (4, 5, 6)]
    mean = ahead + behind
    lane = lax.broadcasted_iota(jnp.int32, (rows, quarter), 1)
    scales[:, :SEG] = half[:, :SEG]
    scales[:, SEG:SEG + quarter] = mean
    scales[:, SEG + quarter:SEG + HALF] = jnp.where(lane == 0, 2.0 * last, mean)
    scales[:, SEG + HALF:] = ahead - behind

    for i in range(parts):
        copies[i].wait()
        for k in range(2):
            weights[k, :, pl.ds(i * width, width)] = raw[i, k].astype(F32) * (1.0 / 2048.0)
    copies[parts].wait()


def main_kernel(
    arrived, others, weights, onehot, scales, tables_in, *refs,
):
    sides, (out, window, mhl, x, f, total) = refs[:-6], refs[-6:]
    groups = lax.axis_size("group")
    times = lax.axis_size("tm")
    width = arrived.shape[3]
    rows = weights.shape[1]
    blocks = weights.shape[2] // LANES
    tile_blocks = groups * times * width
    depth = mhl.shape[0]
    local = 3 * tile_blocks
    segs = blocks // PER_SEG
    halves = 2
    chunk_segs = segs // halves
    chunk_blocks = chunk_segs * PER_SEG
    chunk = chunk_blocks * rows
    tiles = (1, tile_sides(1)[0], tile_sides(0)[0])

    window[...] = jnp.zeros(window.shape, F32)
    for k in range(times):
        core = source_of("tm", k)
        if times == 2:
            near = jnp.where(core == 0, tile_sides(1)[0], tile_sides(0)[0])
            spots = [(1, core), (near, core), (near, 1 - core)]
        else:
            spots = [(tile, core) for tile in tiles]
        for j in range(groups):
            for s, (tile, share) in enumerate(spots):
                at = tile * tile_blocks + (source_of("group", j) * times + share) * width
                place = pl.ds(pl.multiple_of(at, 8), width)
                for c in range(3):
                    piece = arrived[j, s, c] if k == 0 else others[k - 1, j, s, c]
                    window[place, pl.ds(c * LANES, LANES)] = piece
    mhl[:, :3 * LANES], mhl[:, 3 * LANES:] = split(window[...])

    ids = lax.broadcasted_iota(jnp.int32, (rows, depth), 1).astype(F32)

    def scan(picked, j, q, u):
        part = picked[j * rows:(j + 1) * rows]
        return part[:, :LANES] + q * part[:, LANES:2 * LANES] + u * part[:, 2 * LANES:]

    upper_at = (segs + 1) * rows
    for at in (0, upper_at):
        x[pl.ds(at, rows), :] = jnp.zeros((rows, SEG), F32)
    if len(sides) == 1:
        places = (jnp.where(lax.axis_index("tm") == 0, upper_at, 0),)
    else:
        places = (0, upper_at)
    for side, at in zip(sides, places):
        flags = side[2 * PER_SEG] - 1.0
        ones = jnp.concatenate(
            [
                jnp.where(jnp.broadcast_to(flags[:, j:j + 1], (rows, depth)) == ids, 1.0, 0.0)
                for j in range(PER_SEG)
            ],
            axis=0,
        ).astype(BF)
        picked = dot(ones, mhl[...])
        picked = picked[:, :3 * LANES] + picked[:, 3 * LANES:]
        place = pl.ds(at if isinstance(at, int) else pl.multiple_of(at, rows), rows)
        for j in range(PER_SEG):
            x[place, pl.ds(j * LANES, LANES)] = scan(picked, j, side[j], side[PER_SEG + j])

    def scan_part(i):
        ones = onehot[i * chunk:(i + 1) * chunk, :]
        picked = dot(ones, mhl[...])
        picked = picked[:, :3 * LANES] + picked[:, 3 * LANES:]
        for j in range(chunk_blocks):
            lanes = pl.ds((i * chunk_blocks + j) * LANES, LANES)
            at = (i * chunk_segs + 1 + j // PER_SEG) * rows
            x[pl.ds(at, rows), pl.ds((j % PER_SEG) * LANES, LANES)] = scan(
                picked, j, weights[0, :, lanes], weights[1, :, lanes]
            )

    g1h, g1l = tables_in[:HALF, :HALF], tables_in[:HALF, HALF:]
    g2h, g2l = tables_in[HALF:SEG, :HALF], tables_in[HALF:SEG, HALF:]
    turn = tables_in[SEG:, :].astype(F32)
    turn = turn[:, :HALF] + turn[:, HALF:]
    cos, sin = turn[:1], turn[16:17]
    quarter = HALF // 2
    part = chunk_segs * rows

    def weighted(coeffs, at, width):
        scale = scales[:, at:at + width]
        return (coeffs.reshape(chunk_segs, rows, width) * scale[None]).reshape(part, width)

    def forward(i):
        base = i * part
        middle = x[pl.ds(base + rows, part), :]
        around = 0.5 * (x[pl.ds(base, part), :] + x[pl.ds(base + 2 * rows, part), :])
        even = middle + around
        odd = middle - around
        real = cos * odd[:, :HALF] - sin * odd[:, HALF:]
        imag = sin * odd[:, :HALF] + cos * odd[:, HALF:]
        most = jnp.concatenate([even[:, :HALF] + even[:, HALF:], real, imag], axis=0)
        return (
            dot3(dot, even[:, :HALF] - even[:, HALF:], g2h, g2l),
            dot3(dot, most, g1h, g1l),
        )

    def scaled(found):
        second, coeffs = found
        real, imag = coeffs[part:2 * part], coeffs[2 * part:]
        near, far = slice(None, quarter), slice(quarter, None)
        cross = SEG + HALF
        turned_real = [
            weighted(real[:, near], SEG, quarter) - weighted(imag[:, far], cross, quarter),
            weighted(real[:, far], SEG + quarter, quarter) + weighted(imag[:, near], cross, quarter),
        ]
        turned_imag = [
            weighted(imag[:, near], SEG, quarter) + weighted(real[:, far], cross, quarter),
            weighted(imag[:, far], SEG + quarter, quarter) - weighted(real[:, near], cross, quarter),
        ]
        most = [weighted(coeffs[:part], 0, HALF)]
        most += [jnp.concatenate(turned, axis=1) for turned in (turned_real, turned_imag)]
        return weighted(second, HALF, HALF), jnp.concatenate(most, axis=0)

    def backward(i, coeffs):
        second = dot3(dot_t, coeffs[0], g2h, g2l)
        back = dot3(dot_t, coeffs[1], g1h, g1l)
        first, real, imag = back[:part], back[part:2 * part], back[2 * part:]
        place = pl.ds(i * part, part)
        f[place, :HALF] = first + second + cos * real + sin * imag
        f[place, HALF:] = first - second - sin * real + cos * imag

    def bin_part(i):
        values = []
        for j in range(chunk_blocks):
            lanes = pl.ds((i * chunk_blocks + j) * LANES, LANES)
            at = (i * chunk_segs + j // PER_SEG) * rows
            value = f[pl.ds(at, rows), pl.ds((j % PER_SEG) * LANES, LANES)]
            values.append(
                jnp.concatenate(
                    [value, weights[0, :, lanes] * value, weights[1, :, lanes] * value], axis=1
                )
            )
        sums = lax.dot_general(
            onehot[i * chunk:(i + 1) * chunk, :local],
            jnp.concatenate(split(jnp.concatenate(values, axis=0)), axis=1),
            (((0,), (0,)), ((), ())),
            preferred_element_type=F32,
        )
        return sums[:, :3 * LANES] + sums[:, 3 * LANES:]

    scan_part(0)
    found = []
    for i in range(1, halves):
        scan_part(i)
        found.append(forward(i - 1))
    found.append(forward(halves - 1))
    sums = []
    for i in range(halves):
        backward(i, scaled(found[i]))
        if i:
            sums.append(bin_part(i - 1))
    sums.append(bin_part(halves - 1))
    total[...] = sum(sums)
    tiles = (1, tile_sides(0)[1], tile_sides(1)[1])
    for k in range(times):
        for s in range(3):
            for g in range(groups):
                at = tiles[s] * tile_blocks + (g * times + target_of("tm", k)) * width
                out[k, s, g] = total[pl.ds(pl.multiple_of(at, 8), width), :]


def sum_kernel(arrived, parts, image, sums):
    groups = arrived.shape[0]
    rows = [jnp.zeros((1, LANES), F32)] * 4
    for j in range(groups):
        g = source_of("group", j)
        pixels = parts[0, g]
        for k in range(1, groups):
            pixels = pixels + parts[k, g]
        for c in range(3):
            a = pixels[:, c * LANES:(c + 1) * LANES]
            d = arrived[j, 0, c]
            r = arrived[j, 3, c]
            if j == 0:
                image[c] = a
            for i, term in enumerate((r * r, d * a, r * a, a * a)):
                rows[i] = rows[i] + jnp.sum(term, axis=0, keepdims=True)
    sums[...] = jnp.concatenate(rows + [jnp.zeros((4, LANES), F32)], axis=0)


def step_kernel(sums, image, arrived, solution_in, new_solution, new_residual, new_direction):
    old_norm, curvature, cross_term, image_norm = [
        jnp.sum(sums[i:i + 1, :], axis=1, keepdims=True) for i in range(4)
    ]
    step_size = old_norm / curvature
    new_norm = old_norm - 2.0 * step_size * cross_term + step_size * step_size * image_norm
    ratio = new_norm / old_norm
    for c in range(3):
        d = arrived[0, 0, c]
        residual = arrived[0, 3, c] - step_size * image[c]
        new_solution[c, 0] = solution_in[c, 0] + step_size * d
        new_residual[c, 0] = residual
        new_direction[c, 0] = residual + ratio * d


def copy_kernel(source, target):
    target[...] = source[:, 0]


def vmem_call(kernel, out_shape, args, scratch=(), limit=24):
    spec = pl.BlockSpec(memory_space=pltpu.VMEM)
    return pl.pallas_call(
        kernel,
        out_shape=out_shape,
        in_specs=[spec] * len(args),
        out_specs=jax.tree.map(lambda _: spec, out_shape),
        scratch_shapes=list(scratch),
        compiler_params=pltpu.CompilerParams(vmem_limit_bytes=limit * 2**20),
    )(*args)


def edges(hits, stokes_int, map_residual, count):
    rows, blocks = hits.shape
    edge = jax.ShapeDtypeStruct((2 * PER_SEG + 1, rows, blocks), F32)
    spec = pl.BlockSpec(memory_space=pltpu.VMEM)
    return pl.pallas_call(
        functools.partial(edge_kernel, count),
        out_shape=[edge] * count + [jax.ShapeDtypeStruct(map_residual[:, 0].shape, F32)],
        in_specs=[spec, pl.BlockSpec(memory_space=pl.ANY), spec],
        out_specs=[spec] * (count + 1),
        scratch_shapes=[
            pltpu.VMEM((count, 2, rows, SEG), jnp.int32),
            pltpu.SemaphoreType.DMA((count,)),
        ],
        compiler_params=pltpu.CompilerParams(vmem_limit_bytes=32 * 2**20),
        cost_estimate=pl.CostEstimate(flops=0, bytes_accessed=8 * 10**6, transcendentals=0),
    )(hits, stokes_int, map_residual)


def prepare(payload, hits, stokes_int, inv_noise, depth):
    rows, samples = stokes_int.shape[1:]
    blocks = samples // LANES
    fixed = table_rows()
    parts = 4
    out_shape = [
        jax.ShapeDtypeStruct(payload.shape, F32),
        jax.ShapeDtypeStruct(stokes_int.shape, F32),
        jax.ShapeDtypeStruct((rows * blocks, depth), BF),
        jax.ShapeDtypeStruct((rows, 3 * HALF + HALF // 2), F32),
        jax.ShapeDtypeStruct(fixed.shape, BF),
    ]
    spec = pl.BlockSpec(memory_space=pltpu.VMEM)
    far = pl.BlockSpec(memory_space=pl.ANY)
    return pl.pallas_call(
        prep_kernel,
        out_shape=out_shape,
        in_specs=[spec, spec, spec, far, far],
        out_specs=[spec] * len(out_shape),
        scratch_shapes=[
            pltpu.VMEM((parts, 2, rows, samples // parts), jnp.int32),
            pltpu.SemaphoreType.DMA((parts + 1,)),
        ],
        compiler_params=pltpu.CompilerParams(vmem_limit_bytes=32 * 2**20),
        cost_estimate=pl.CostEstimate(flops=0, bytes_accessed=12 * 10**6, transcendentals=0),
    )(payload, hits, inv_noise, stokes_int, fixed)


def exchanged(value, axis):
    return [value] + [
        lax.ppermute(value, axis, partner_perm(axis, by)) for by in range(1, lax.axis_size(axis))
    ]


def summed(value, axis):
    count = lax.axis_size(axis)
    if count & (count - 1):
        return sum(exchanged(value, axis))
    by = 1
    while by < count:
        value = value + lax.ppermute(value, axis, partner_perm(axis, by))
        by *= 2
    return value


def det_sum(value):
    count = lax.axis_size("det")
    if lax.axis_size("tm") != 2 or count < 4 or count & (count - 1):
        return sum(exchanged(value, "det"))
    fetched = 0.0
    for by in range(1, count // 2):
        mixed = [(2 * z + t, 2 * (z ^ (count - by if t else by)) + t) for z in range(count) for t in range(2)]
        fetched = fetched + lax.ppermute(value, ("det", "tm"), mixed)
    across = lax.ppermute(value, "det", partner_perm("det", count // 2))
    return value + across + fetched + lax.ppermute(fetched, "tm", partner_perm("tm", 1))


def shards(map_solution, map_residual, map_direction, hits, stokes_int, inv_noise):
    groups = lax.axis_size("group")
    times = lax.axis_size("tm")
    width = map_direction.shape[2]
    local = 3 * groups * times * width
    depth = -(-local // 256) * 256
    rows = hits.shape[0]
    segs = hits.shape[1] // PER_SEG

    own = map_direction[:, 0]
    if times == 2:
        mixed = [(2 * a + t, 2 * b + t) for t in range(2) for a, b in tile_perm(1 - t)]
        other = lax.ppermute(own, "tm", partner_perm("tm", 1))
        own = vmem_call(copy_kernel, jax.ShapeDtypeStruct(own.shape, F32), [map_direction])
        pair = jnp.stack([own, other])
        near = list(lax.ppermute(pair, ("det", "tm"), mixed))
    else:
        near = [lax.ppermute(own, "det", tile_perm(e)) for e in (1, 0)]
    *edge, residual = edges(hits, stokes_int, map_residual, 1 if times == 2 else 2)
    payload = jnp.stack([own] + near + [residual])
    from_group = exchanged(payload, "group")
    payload, weights, onehot, scales, fixed = prepare(payload, hits, stokes_int, inv_noise, depth)
    arrived = jnp.stack([payload] + from_group[1:])
    if times == 2:
        sent = jnp.concatenate([arrived.reshape(-1, width, LANES), edge[0].reshape(-1, width, LANES)])
        came = lax.ppermute(sent, "tm", partner_perm("tm", 1))
        others = came[:arrived.size // (width * LANES)].reshape((1,) + arrived.shape)
        sides = [came[arrived.size // (width * LANES):].reshape(edge[0].shape)]
    else:
        forward = [(i, i + 1) for i in range(times - 1)]
        backward = [(b, a) for a, b in forward]
        sides = [lax.ppermute(edge[1], "tm", forward), lax.ppermute(edge[0], "tm", backward)]
        others = jnp.stack(exchanged(arrived, "tm")[1:])

    binned = vmem_call(
        main_kernel,
        jax.ShapeDtypeStruct((times, 3, groups, width, 3 * LANES), F32),
        [arrived, others, weights, onehot, scales, fixed] + sides,
        [
            pltpu.VMEM((depth, 3 * LANES), F32),
            pltpu.VMEM((depth, 6 * LANES), BF),
            pltpu.VMEM(((segs + 2) * rows, SEG), F32),
            pltpu.VMEM((segs * rows, SEG), F32),
            pltpu.VMEM((local, 3 * LANES), F32),
        ],
    )
    half = binned[0]
    for by in range(1, times):
        half = half + lax.ppermute(binned[by], "tm", partner_perm("tm", by))
    pixels = half[0]
    for e in range(2):
        pixels = pixels + lax.ppermute(half[1 + e], "det", tile_perm(e))
    parts = jnp.stack(exchanged(pixels, "group"))
    image, sums = vmem_call(
        sum_kernel,
        [
            jax.ShapeDtypeStruct((3, width, LANES), F32),
            jax.ShapeDtypeStruct((8, LANES), F32),
        ],
        [arrived, parts],
    )
    sums = det_sum(summed(sums, "tm"))
    return vmem_call(
        step_kernel,
        [jax.ShapeDtypeStruct(map_solution.shape, F32)] * 3,
        [sums, image, arrived, map_solution],
    )


def solution(mesh):
    map_placed = P(None, "det", ("group", "tm"), None)
    placed = (
        map_placed,
        map_placed,
        map_placed,
        P(("group", "det"), "tm"),
        P(None, ("group", "det"), "tm"),
        P(("group", "det"), None),
    )
    return jax.shard_map(
        shards,
        mesh=mesh,
        in_specs=placed,
        out_specs=(map_placed, map_placed, map_placed),
        check_vma=False,
    )
```
